128 devices in a mesh: ax: 16 (over y, x_hi, core), circ: 8 (over x_lo, z).
Axes of the slice: x: 4 (x_hi: 2, x_lo: 2; x = x_hi * 2 + x_lo), y: 4, z: 4, core: 2. Of those that a mesh axis runs over, the one named last changes fastest.
Arguments:
- endothelium: float32 [3, 64, 1024, 128], P(None, 'ax', 'circ'), may hold values from -6 to 6
- muscle: float32 [3, 128, 512, 128], P(None, 'ax', 'circ'), may hold values from -6 to 6
- agonist: float32 [64, 1024, 128], P('ax', 'circ'), may hold values from 0.2 to 2
- proj_cell: int32 [128, 128, 2], P(('ax', 'circ')), may hold values from 0 to 511
- proj_target: int32 [128, 128, 2], P(('ax', 'circ')), may hold values from 0 to 511
- proj_count: int32 [128, 128], P(('ax', 'circ')), may hold values from 0 to 2, as said below
- endo_inverse: float32 [3, 128, 128], replicated, may hold values from 0 to 0.29
- muscle_inverse: float32 [3, 128, 128], replicated, may hold values from 0 to 0.43
Outputs:
- endo_next: float32 [3, 64, 1024, 128], P(None, 'ax', 'circ')
- muscle_next: float32 [3, 128, 512, 128], P(None, 'ax', 'circ')
The draws below stay inside these ranges and needn't reach their ends.
Inputs may be any that keep to these rules, and one draw needn't show every extreme that they name: `proj_count`: the live slots of a pair are its first ones. In every draw some owner receives 2 from every device and some device sends 2 to every owner.
All inputs are finite; a program needn't handle non-finite values.
Results may differ from the reference program's by a relative error of at most 0.0001.
Values sent between devices are 32-bit elements; how exact they have to be, the bound alone decides.
No kernel may reach another device: no remote copies, remote signals or barrier semaphores. Data moves between devices by JAX's collectives and lax.ppermute only.
A program may use at most 64 MiB of HBM per device.

```python
import math
import jax
import jax.numpy as jnp
from jax import lax

POINTS = 128
ENDO_AX = 4
ENDO_CIRC = 128
MUSC_AX = 8
MUSC_CIRC = 64
PAIR_SLOTS = 2
TIME_STEPS = 8
OWNERS = 128
ENDO_CELLS = 512
MUSC_CELLS = 512
ENDO_LEN = 64
ENDO_CYCLE = 1024
MUSC_LEN = 128
MUSC_CYCLE = 512


def cable_inverse(key, lengths, spread):
    index = jnp.arange(POINTS, dtype=jnp.float32)
    distance = jnp.abs(index[:, None] - index[None, :])
    length_scale = jnp.array(lengths, jnp.float32)[:, None, None]
    ratio = jnp.exp(-1.0 / length_scale)
    total = (1.0 + ratio) / (1.0 - ratio)
    rough = jax.random.uniform(key, (3, POINTS, POINTS), jnp.float32, 1.0 - spread, 1.0 + spread)
    return (jnp.exp(-distance[None] / length_scale) * rough / total).astype(jnp.float32)


def draw_endo_inverse(key, part):
    key = jax.random.fold_in(key, 11)
    return cable_inverse(key, [3.0, 8.0, 24.0], 0.5)


def draw_muscle_inverse(key, part):
    key = jax.random.fold_in(key, 13)
    return cable_inverse(key, [2.0, 6.0, 16.0], 0.5)


def draw_proj_count(key, part):
    key = jax.random.fold_in(key, 7)
    first, second, third = jax.random.split(key, 3)
    base = jax.random.randint(first, (OWNERS, OWNERS), 0, PAIR_SLOTS + 1, dtype=jnp.int32)
    sender = jax.random.randint(second, (), 0, OWNERS, dtype=jnp.int32)
    receiver = jax.random.randint(third, (), 0, OWNERS, dtype=jnp.int32)
    owner_ids = jnp.arange(OWNERS, dtype=jnp.int32)
    filled = (owner_ids[:, None] == sender) | (owner_ids[None, :] == receiver)
    return jnp.where(filled, PAIR_SLOTS, base).astype(jnp.int32)


def with_ends(values, stream_key, low, largest):
    dims = values.shape
    place = [jax.random.randint(jax.random.fold_in(stream_key, axis), (), 0, dims[axis]) for axis in range(len(dims))]
    values = values.at[tuple(place)].set(low)
    longest = dims.index(max(dims))
    place[longest] = (place[longest] + 1) % dims[longest]
    return values.at[tuple(place)].set(largest)


def shard_levels(rng, extent, shards, least, high):
    def one(axis_at, parts):
        draws = jax.random.uniform(jax.random.fold_in(jax.random.fold_in(rng, 6), axis_at), (parts,), jnp.float32, least / len(shards), high / len(shards))
        return jnp.repeat(jnp.exp(draws), extent[axis_at] // parts).reshape((-1,) + (1,) * (len(extent) - axis_at - 1))

    level = one(*shards[0])
    for cut in shards[1:]:
        level = level * one(*cut)
    return level


def normal_values(key, dims, width, limit, shards=(), kind=jnp.bfloat16):
    values = width * jax.random.normal(key, dims, jnp.float32)
    if shards:
        values = values * shard_levels(key, dims, shards, -0.22, 0.18)
    return jnp.clip(values, -limit, limit).astype(kind)


def setup_inputs(seed: int = 0) -> dict:
    splits = jax.random.split(jax.random.key(seed), 9)
    return {
        "endothelium": normal_values(splits[0], (3, ENDO_LEN, ENDO_CYCLE, POINTS), 1.0, 6.0, ((1, 16), (2, 8)), jnp.float32),
        "muscle": normal_values(splits[1], (3, MUSC_LEN, MUSC_CYCLE, POINTS), 1.0, 6.0, ((1, 16), (2, 8)), jnp.float32),
        "agonist": jnp.clip(jnp.exp(math.log(2.0) - 2.3025851 * jax.random.uniform(splits[2], (ENDO_LEN, ENDO_CYCLE, POINTS), jnp.float32) ** shard_levels(splits[2], (ENDO_LEN, ENDO_CYCLE, POINTS), ((0, 16), (1, 8)), -0.2, 0.2)), 0.2, 2.0),
        "proj_cell": with_ends(jax.random.randint(splits[3], (OWNERS, OWNERS, PAIR_SLOTS), 0, ENDO_CELLS), jax.random.fold_in(splits[3], 1), 0, ENDO_CELLS - 1).astype(jnp.int32),
        "proj_target": with_ends(jax.random.randint(splits[4], (OWNERS, OWNERS, PAIR_SLOTS), 0, MUSC_CELLS), jax.random.fold_in(splits[4], 1), 0, MUSC_CELLS - 1).astype(jnp.int32),
        "proj_count": draw_proj_count(jax.random.fold_in(splits[8], 71), 0),
        "endo_inverse": draw_endo_inverse(jax.random.fold_in(splits[8], 71), 0),
        "muscle_inverse": draw_muscle_inverse(jax.random.fold_in(splits[8], 71), 0),
    }


time_step = 0.2


def reaction(current, stimulus):
    calcium = current[0]
    inositol = current[1]
    voltage = current[2]
    release = inositol * inositol / (0.5 + inositol * inositol)
    return jnp.stack([1.2 * release - 0.6 * calcium - 0.2 * voltage,
                      stimulus - 0.5 * inositol,
                      0.5 * calcium - 0.8 * voltage])


def owner_rows(field, tile_axial, tile_cycle):
    species, length, cycle, points = field.shape
    blocks = field.reshape(species, length // tile_axial, tile_axial, cycle // tile_cycle, tile_cycle, points)
    return blocks.transpose(0, 1, 3, 2, 4, 5).reshape(species, -1, points)


def field_rows(rows, length, cycle, tile_axial, tile_cycle):
    species = rows.shape[0]
    points = rows.shape[2]
    blocks = rows.reshape(species, length // tile_axial, cycle // tile_cycle, tile_axial, tile_cycle, points)
    return blocks.transpose(0, 1, 3, 2, 4, 5).reshape(species, length, cycle, points)


def reference(endothelium, muscle, agonist, proj_cell, proj_target, proj_count, endo_inverse, muscle_inverse):
    owner_ids = jnp.arange(OWNERS, dtype=jnp.int32)
    endo_index = (owner_ids[:, None, None] * ENDO_CELLS + proj_cell).reshape(-1)
    muscle_index = (owner_ids[None, :, None] * MUSC_CELLS + proj_target).reshape(-1)
    slot_ids = jnp.arange(PAIR_SLOTS, dtype=jnp.int32)
    live_slot = (slot_ids[None, None, :] < proj_count[:, :, None]).astype(jnp.float32).reshape(-1)[None, :, None]
    coupling = jnp.array([0.1, 0.3, 0.5], jnp.float32)[:, None, None]
    endo_gap = jnp.array([0.05, 0.3, 0.5], jnp.float32)[:, None, None, None]
    muscle_gap = jnp.array([0.05, 0.1, 0.4], jnp.float32)[:, None, None, None]
    current_endo = endothelium
    current_muscle = muscle
    for step_index in range(TIME_STEPS):
        endo_rows = owner_rows(current_endo, ENDO_AX, ENDO_CIRC)
        muscle_rows = owner_rows(current_muscle, MUSC_AX, MUSC_CIRC)
        flux = coupling * (endo_rows[:, endo_index] - muscle_rows[:, muscle_index]) * live_slot
        endo_gain = field_rows(jnp.zeros_like(endo_rows).at[:, endo_index].add(-flux), ENDO_LEN, ENDO_CYCLE, ENDO_AX, ENDO_CIRC)
        muscle_gain = field_rows(jnp.zeros_like(muscle_rows).at[:, muscle_index].add(flux), MUSC_LEN, MUSC_CYCLE, MUSC_AX, MUSC_CIRC)
        endo_pad = jnp.pad(current_endo, ((0, 0), (1, 1), (0, 0), (0, 0)))
        endo_lap = endo_pad[:, 2:] + endo_pad[:, :-2] - 2.0 * current_endo
        muscle_lap = jnp.roll(current_muscle, 1, axis=2) + jnp.roll(current_muscle, -1, axis=2) - 2.0 * current_muscle
        endo_rhs = current_endo + time_step * (reaction(current_endo, agonist) + endo_gap * endo_lap + endo_gain)
        muscle_rhs = current_muscle + time_step * (reaction(current_muscle, 0.0) + muscle_gap * muscle_lap + muscle_gain)
        current_endo = jnp.einsum("sawj,sij->sawi", endo_rhs, endo_inverse, precision=lax.Precision.HIGHEST)
        current_muscle = jnp.einsum("sawj,sij->sawi", muscle_rhs, muscle_inverse, precision=lax.Precision.HIGHEST)
    return current_endo, current_muscle
```

```python
import functools

import jax
import jax.numpy as jnp
from jax import lax
from jax.experimental import pallas as pl
from jax.experimental.pallas import tpu as pltpu
from jax.sharding import PartitionSpec as P

TIME_STEPS = 8
TIME_STEP = 0.2
COUPLING = (0.1, 0.3, 0.5)
ENDO_GAP = (0.05, 0.3, 0.5)
MUSCLE_GAP = (0.05, 0.1, 0.4)
DEVICES = ("ax", "circ")
PAIR = 2
SPECIES = 3
POINTS = 128
CELLS = 512
OWNERS = 128
HALF = SPECIES * PAIR * POINTS
WIDE = SPECIES * POINTS
VMEM_LIMIT = 40 * 1024 * 1024


def col(i):
    return slice(i * POINTS, (i + 1) * POINTS)


def halves(x):
    hi = x.astype(jnp.bfloat16)
    lo = (x - hi.astype(jnp.float32)).astype(jnp.bfloat16)
    return hi, lo


def dot(a, b):
    return jnp.dot(a, b, preferred_element_type=jnp.float32)


def pick_rows(pick, parts, out, base):
    rows = dot(pick[...], parts[...])
    for s in range(SPECIES):
        value = rows[:, col(s)] + rows[:, col(SPECIES + s)]
        for k in range(PAIR):
            out[:, base + (s * PAIR + k) * POINTS : base + (s * PAIR + k + 1) * POINTS] = value[
                k * OWNERS : (k + 1) * OWNERS
            ]


def store_parts(parts, s, rows, value):
    hi, lo = halves(value)
    parts[rows, col(s)] = hi
    parts[rows, col(SPECIES + s)] = lo


def flux_parts(recv, recv_base, sent, sent_base, parts):
    for s in range(SPECIES):
        for k in range(PAIR):
            at = (s * PAIR + k) * POINTS
            flux = (
                recv[:, recv_base + at : recv_base + at + POINTS]
                - sent[:, sent_base + at : sent_base + at + POINTS]
            )
            store_parts(parts, s, slice(k * OWNERS, (k + 1) * OWNERS), flux)


def rates(u0, u1, u2, drive):
    square = u1 * u1
    release = square / (0.5 + square)
    return (
        1.2 * release - 0.6 * u0 - 0.2 * u2,
        drive - 0.5 * u1,
        0.5 * u0 - 0.8 * u2,
    )


def first_kernel(e, m, te, tm, out, parts):
    for field, pick, base in ((e, te, 0), (m, tm, HALF)):
        for s in range(SPECIES):
            store_parts(parts, s, slice(None), field[s])
        pick_rows(pick, parts, out, base)


def step_kernel(
    last, e, m, ag, recv, sent, eu, ed, ml, mr, se, sm, te, tm, we, wm, *rest
):
    if last:
        e_new, m_new, flux, gain, stacked = rest
    else:
        e_new, m_new, send, e_top, e_bot, m_lo, m_hi, flux, gain, stacked, parts = rest
    flux_parts(recv, HALF, sent, 0, flux)
    gain[...] = dot(se[...], flux[...])
    for c in range(4):
        rows = slice(c * 128, (c + 1) * 128)
        u = [e[s, rows] for s in range(SPECIES)]
        rate = rates(*u, ag[rows])
        for s in range(SPECIES):
            before = eu[s] if c == 0 else e[s, (c - 1) * 128 : c * 128]
            after = ed[s] if c == 3 else e[s, (c + 1) * 128 : (c + 2) * 128]
            lap = before + after - 2.0 * u[s]
            total = gain[rows, col(s)] + gain[rows, col(SPECIES + s)]
            rhs = u[s] + TIME_STEP * (rate[s] + ENDO_GAP[s] * lap + COUPLING[s] * total)
            hi, lo = halves(rhs)
            stacked[s, rows, 0:POINTS] = hi
            stacked[s, rows, POINTS:] = lo
    for s in range(SPECIES):
        wide = dot(stacked[s], we[s])
        value = wide[:, :POINTS] + wide[:, POINTS:]
        e_new[s] = value
        if not last:
            e_top[s] = value[0:128]
            e_bot[s] = value[384:512]
            store_parts(parts, s, slice(None), value)
    if not last:
        pick_rows(te, parts, send, 0)
    flux_parts(recv, 0, sent, HALF, flux)
    gain[...] = dot(sm[...], flux[...])
    place = lax.broadcasted_iota(jnp.int32, (64, POINTS), 0)
    for c in range(8):
        rows = slice(c * 64, (c + 1) * 64)
        u = [m[s, rows] for s in range(SPECIES)]
        rate = rates(*u, 0.0)
        for s in range(SPECIES):
            before = jnp.where(place == 0, ml[s, c : c + 1], pltpu.roll(u[s], 1, 0))
            after = jnp.where(place == 63, mr[s, c : c + 1], pltpu.roll(u[s], 63, 0))
            lap = before + after - 2.0 * u[s]
            total = gain[rows, col(s)] + gain[rows, col(SPECIES + s)]
            rhs = u[s] + TIME_STEP * (rate[s] + MUSCLE_GAP[s] * lap + COUPLING[s] * total)
            hi, lo = halves(rhs)
            stacked[s, rows, 0:POINTS] = hi
            stacked[s, rows, POINTS:] = lo
    for s in range(SPECIES):
        wide = dot(stacked[s], wm[s])
        value = wide[:, :POINTS] + wide[:, POINTS:]
        m_new[s] = value
        if not last:
            for c in range(8):
                m_lo[s, c : c + 1] = value[c * 64 : c * 64 + 1]
                m_hi[s, c : c + 1] = value[c * 64 + 63 : c * 64 + 64]
            store_parts(parts, s, slice(None), value)
    if not last:
        pick_rows(tm, parts, send, HALF)


def f32(*shape):
    return jax.ShapeDtypeStruct(shape, jnp.float32)


def vmem():
    return pl.BlockSpec(memory_space=pltpu.VMEM)


def first_call(e, m, te, tm):
    return pl.pallas_call(
        first_kernel,
        out_shape=f32(OWNERS, 2 * HALF),
        in_specs=[vmem()] * 4,
        out_specs=vmem(),
        scratch_shapes=[pltpu.VMEM((CELLS, 2 * WIDE), jnp.bfloat16)],
        compiler_params=pltpu.CompilerParams(vmem_limit_bytes=VMEM_LIMIT),
        name="first_rows",
    )(e, m, te, tm)


def step_call(last, args):
    outs = [f32(SPECIES, CELLS, POINTS)] * 2
    if not last:
        outs += [f32(OWNERS, 2 * HALF)]
        outs += [f32(SPECIES, 128, POINTS)] * 2 + [f32(SPECIES, 8, POINTS)] * 2
    scratch = [
        pltpu.VMEM((PAIR * OWNERS, 2 * WIDE), jnp.bfloat16),
        pltpu.VMEM((CELLS, 2 * WIDE), jnp.float32),
        pltpu.VMEM((SPECIES, CELLS, 2 * POINTS), jnp.bfloat16),
    ]
    if not last:
        scratch += [pltpu.VMEM((CELLS, 2 * WIDE), jnp.bfloat16)]
    return pl.pallas_call(
        functools.partial(step_kernel, last),
        out_shape=outs,
        in_specs=[vmem()] * len(args),
        out_specs=[vmem()] * len(outs),
        scratch_shapes=scratch,
        compiler_params=pltpu.CompilerParams(vmem_limit_bytes=VMEM_LIMIT),
        name="last_step" if last else "step",
    )(*args)


def weights(inverse):
    turned = inverse.transpose(0, 2, 1)
    rounded = lax.reduce_precision(turned, 8, 7)
    hi = rounded.astype(jnp.bfloat16)
    lo = (turned - rounded).astype(jnp.bfloat16)
    row = jnp.concatenate([hi, lo], axis=2)
    return jnp.concatenate([row, row], axis=1)


def one_hot(index):
    flat = index.T.reshape(-1)
    cells = jnp.arange(CELLS, dtype=jnp.int32)
    spread = (cells[:, None] == flat[None, :]).astype(jnp.bfloat16)
    pick = (flat[:, None] == cells[None, :]).astype(jnp.bfloat16)
    return spread, pick


def around(x, axis, step, closed):
    count = lax.axis_size(axis)
    pairs = [
        (i, (i + step) % count) for i in range(count) if closed or 0 <= i + step < count
    ]
    return lax.ppermute(x, axis, pairs)


def local(
    endothelium, muscle, agonist, proj_cell, proj_target, proj_count, endo_inverse, muscle_inverse
):
    e = endothelium.reshape(SPECIES, CELLS, POINTS)
    m = muscle.reshape(SPECIES, CELLS, POINTS)
    ag = agonist.reshape(CELLS, POINTS)
    slot_ids = jnp.arange(PAIR, dtype=jnp.int32)
    live = slot_ids[None, :] < proj_count[0][:, None]
    arrived = lax.all_to_all(
        jnp.where(live, proj_target[0], -1), DEVICES, split_axis=0, concat_axis=0, tiled=True
    )
    se, te = one_hot(jnp.where(live, proj_cell[0], -1))
    sm, tm = one_hot(arrived)
    we = weights(endo_inverse)
    wm = weights(muscle_inverse)
    sent = first_call(e, m, te, tm)
    e_top, e_bot = endothelium[:, 0], endothelium[:, 3]
    m_lo, m_hi = muscle[:, :, 0], muscle[:, :, 63]
    for step in range(TIME_STEPS):
        recv = lax.all_to_all(sent, DEVICES, split_axis=0, concat_axis=0, tiled=True)
        eu = around(e_bot, "ax", 1, False)
        ed = around(e_top, "ax", -1, False)
        ml = around(m_hi, "circ", 1, True)
        mr = around(m_lo, "circ", -1, True)
        last = step == TIME_STEPS - 1
        res = step_call(
            last, (e, m, ag, recv, sent, eu, ed, ml, mr, se, sm, te, tm, we, wm)
        )
        if last:
            e, m = res
        else:
            e, m, sent, e_top, e_bot, m_lo, m_hi = res
    return e.reshape(endothelium.shape), m.reshape(muscle.shape)


def solution(mesh):
    placed = (
        P(None, "ax", "circ", None),
        P(None, "ax", "circ", None),
        P("ax", "circ", None),
        P(("ax", "circ"), None, None),
        P(("ax", "circ"), None, None),
        P(("ax", "circ"), None),
        P(),
        P(),
    )
    return jax.shard_map(
        local,
        mesh=mesh,
        in_specs=placed,
        out_specs=(P(None, "ax", "circ", None), P(None, "ax", "circ", None)),
        check_vma=False,
    )
```

```python
import functools

import jax
import jax.numpy as jnp
from jax import lax
from jax.experimental import pallas as pl
from jax.experimental.pallas import tpu as pltpu
from jax.sharding import PartitionSpec as P

TIME_STEPS = 8
TIME_STEP = 0.2
COUPLING = (0.1, 0.3, 0.5)
ENDO_GAP = (0.05, 0.3, 0.5)
MUSCLE_GAP = (0.05, 0.1, 0.4)
DEVICES = ("ax", "circ")
PAIR = 2
SPECIES = 3
POINTS = 128
CELLS = 512
OWNERS = 128
HALF = SPECIES * PAIR
BLOCKS = 2 * HALF
SLOTS = PAIR * OWNERS
ENDO_SLOTS = SLOTS + 256
MUSCLE_SLOTS = SLOTS + 128
WIDE = SPECIES * POINTS
VMEM_LIMIT = 60 * 1024 * 1024


def col(i):
    return slice(i * POINTS, (i + 1) * POINTS)


def halves(x):
    hi = x.astype(jnp.bfloat16)
    lo = (x - hi.astype(jnp.float32)).astype(jnp.bfloat16)
    return hi, lo


def dot(a, b):
    return jnp.dot(a, b, preferred_element_type=jnp.float32)


def store_parts(parts, s, rows, value):
    hi, lo = halves(value)
    parts[rows, col(s)] = hi
    parts[rows, col(SPECIES + s)] = lo


def both(wide, s):
    return wide[:, col(s)] + wide[:, col(SPECIES + s)]


def slot_rows(base, s, k):
    return pl.ds(base + s * PAIR + k, OWNERS, stride=BLOCKS)


def local_rhs(u, near, drive, deg, gaps):
    decay = (0.6, 0.5, 0.8)
    square = u[1] * u[1]
    release = square / (0.5 + square)
    own = [
        u[s]
        * ((1.0 - TIME_STEP * (decay[s] + 2.0 * gaps[s])) - (TIME_STEP * COUPLING[s]) * deg)
        + (TIME_STEP * gaps[s]) * near[s]
        for s in range(SPECIES)
    ]
    own[0] = own[0] + (TIME_STEP * 1.2) * release - (TIME_STEP * 0.2) * u[2]
    if drive is not None:
        own[1] = own[1] + TIME_STEP * drive
    own[2] = own[2] + (TIME_STEP * 0.5) * u[0]
    return own


def stack(stacked, s, rows, value):
    hi, lo = halves(value)
    stacked[s, rows, 0:POINTS] = hi
    stacked[s, rows, POINTS:] = lo


def mover(sems):
    used = []

    def start(source, dest):
        copy = pltpu.make_async_copy(source, dest, sems.at[len(used)])
        used.append(copy)
        copy.start()
        return copy

    return start


def through(stacked, weight, gaps, parts):
    count = stacked.shape[1]
    for s in range(SPECIES):
        wide = dot(stacked[s], weight[s])
        value = wide[:, :POINTS] + wide[:, POINTS:]
        store_parts(parts, s, slice(0, SLOTS), value[:SLOTS] * (TIME_STEP * COUPLING[s]))
        store_parts(parts, s, slice(SLOTS, count), value[SLOTS:] * (TIME_STEP * gaps[s]))


def endo_slots(recv, eu, ed, stacked):
    for s in range(SPECIES):
        for k in range(PAIR):
            rows = slice(k * OWNERS, (k + 1) * OWNERS)
            stack(stacked, s, rows, recv[slot_rows(HALF, s, k), :])
        stack(stacked, s, slice(SLOTS, SLOTS + 128), eu[s])
        stack(stacked, s, slice(SLOTS + 128, SLOTS + 256), ed[s])


def muscle_slots(recv, ml, mr, stacked):
    for s in range(SPECIES):
        for k in range(PAIR):
            rows = slice(k * OWNERS, (k + 1) * OWNERS)
            stack(stacked, s, rows, recv[slot_rows(0, s, k), :])
        both_ends = jnp.concatenate([ml[s], mr[s]], axis=0)
        stack(stacked, s, slice(SLOTS, SLOTS + 16), both_ends)
        stacked[s, SLOTS + 16 : MUSCLE_SLOTS, :] = jnp.zeros(
            (MUSCLE_SLOTS - SLOTS - 16, 2 * POINTS), jnp.bfloat16
        )


def first_kernel(e_h, m_h, te_h, tm_h, send_h, e, m, te, tm, parts, send, sems):
    start = mover(sems)
    into = [start(a, b) for a, b in ((e_h, e), (te_h, te), (m_h, m), (tm_h, tm))]
    for field, pick, base, ready in ((e, te, 0, into[:2]), (m, tm, HALF, into[2:])):
        for copy in ready:
            copy.wait()
        for s in range(SPECIES):
            store_parts(parts, s, slice(None), field[s])
        rows = dot(pick[...], parts[...])
        for s in range(SPECIES):
            value = both(rows, s)
            for k in range(PAIR):
                send[slot_rows(base, s, k), :] = value[k * OWNERS : (k + 1) * OWNERS]
    start(send, send_h).wait()


def post_kernel(
    recv_h, eu_h, ed_h, ml_h, mr_h, we_h, wm_h, pe_h, pm_h, pge_h, pgm_h,
    send_h, ze_h, zm_h, et_h, eb_h, mlo_h, mhi_h,
    recv, eu, ed, ml, mr, we, wm, pe, pm, pge, pgm, send, ze, zm, et, eb, mlo, mhi,
    stacked_e, stacked_m, sems,
):
    start = mover(sems)
    c_recv, c_eu, c_ed, c_we, c_pe, c_pge, c_ml, c_mr, c_wm, c_pm, c_pgm = [
        start(a, b)
        for a, b in (
            (recv_h, recv), (eu_h, eu), (ed_h, ed), (we_h, we), (pe_h, pe), (pge_h, pge),
            (ml_h, ml), (mr_h, mr), (wm_h, wm), (pm_h, pm), (pgm_h, pgm),
        )
    ]
    outs = []
    c_recv.wait()
    c_eu.wait()
    c_ed.wait()
    endo_slots(recv, eu, ed, stacked_e)
    c_we.wait()
    through(stacked_e, we, ENDO_GAP, ze)
    outs.append(start(ze, ze_h))
    c_pe.wait()
    rows = dot(pe[0:SLOTS], ze[...])
    c_pge.wait()
    for s in range(SPECIES):
        value = both(rows, s) + pge[0:SLOTS, col(s)]
        for k in range(PAIR):
            send[slot_rows(0, s, k), :] = value[k * OWNERS : (k + 1) * OWNERS]
    c_ml.wait()
    c_mr.wait()
    muscle_slots(recv, ml, mr, stacked_m)
    c_wm.wait()
    through(stacked_m, wm, MUSCLE_GAP, zm)
    outs.append(start(zm, zm_h))
    c_pm.wait()
    rows = dot(pm[...], zm[...])
    c_pgm.wait()
    for s in range(SPECIES):
        value = both(rows, s) + pgm[:, col(s)]
        for k in range(PAIR):
            send[slot_rows(HALF, s, k), :] = value[k * OWNERS : (k + 1) * OWNERS]
        mlo[s] = value[SLOTS : SLOTS + 8]
        mhi[s] = value[SLOTS + 8 : SLOTS + 16]
    outs.append(start(send, send_h))
    outs.append(start(mlo, mlo_h))
    outs.append(start(mhi, mhi_h))
    rows = dot(pe[SLOTS:], ze[...])
    for s in range(SPECIES):
        value = both(rows, s) + pge[SLOTS:, col(s)]
        et[s] = value[:128]
        eb[s] = value[128:]
    outs.append(start(et, et_h))
    outs.append(start(eb, eb_h))
    for copy in outs:
        copy.wait()


def last_kernel(
    recv_h, eu_h, ed_h, ml_h, mr_h, we_h, wm_h, se_h, sm_h, be_h, bm_h,
    e_h, m_h,
    recv, eu, ed, ml, mr, we, wm, se, sm, be, bm, ze, zm, stacked_e, stacked_m, sems,
):
    start = mover(sems)
    into = [
        start(a, b)
        for a, b in (
            (recv_h, recv), (eu_h, eu), (ed_h, ed), (we_h, we), (se_h, se), (be_h, be),
            (ml_h, ml), (mr_h, mr), (wm_h, wm), (sm_h, sm), (bm_h, bm),
        )
    ]
    for copy in into[:6]:
        copy.wait()
    endo_slots(recv, eu, ed, stacked_e)
    through(stacked_e, we, ENDO_GAP, ze)
    gain = dot(se[...], ze[...])
    for s in range(SPECIES):
        be[s] = be[s] + both(gain, s)
    out_e = start(be, e_h)
    for copy in into[6:]:
        copy.wait()
    muscle_slots(recv, ml, mr, stacked_m)
    through(stacked_m, wm, MUSCLE_GAP, zm)
    gain = dot(sm[...], zm[...])
    for s in range(SPECIES):
        bm[s] = bm[s] + both(gain, s)
    out_m = start(bm, m_h)
    out_e.wait()
    out_m.wait()


def local_kernel(first, *refs):
    start = mover(refs[-1])
    count = 2 if first else 4
    fields, refs = refs[:count], refs[count:-1]
    (ag_h, se_h, sm_h, te_h, tm_h, we_h, wm_h,
     be_h, bm_h, pge_h, pgm_h,
     e, m, ze, zm, ag, se, sm, te, tm, we, wm, be, bm, pge, pgm, stacked, parts, deg) = refs
    c_e = start(fields[0], e)
    c_se = start(se_h, se)
    if not first:
        c_ze = start(fields[2], ze)
    c_ag, c_we, c_te, c_m, c_sm = [
        start(a, b)
        for a, b in ((ag_h, ag), (we_h, we), (te_h, te), (fields[1], m), (sm_h, sm))
    ]
    if not first:
        c_zm = start(fields[3], zm)
    c_wm = start(wm_h, wm)
    c_tm = start(tm_h, tm)
    ones = jnp.ones((SLOTS, POINTS), jnp.bfloat16)
    outs = []

    def finish(weight, pick, base, pg):
        for s in range(SPECIES):
            wide = dot(stacked[s], weight[s])
            value = wide[:, :POINTS] + wide[:, POINTS:]
            base[s] = value
            store_parts(parts, s, slice(None), value)
        rows = dot(pick[...], parts[...])
        for s in range(SPECIES):
            pg[0:SLOTS, col(s)] = both(rows, s)

    def advance(field, z, spread):
        deg[...] = dot(spread[:, 0:SLOTS], ones)
        if not first:
            gain = dot(spread[...], z[...])
            for s in range(SPECIES):
                field[s] = field[s] + both(gain, s)

    c_e.wait()
    c_se.wait()
    if not first:
        c_ze.wait()
    advance(e, ze, se)
    c_ag.wait()
    for c in range(4):
        rows = slice(c * 128, (c + 1) * 128)
        u = [e[s, rows] for s in range(SPECIES)]
        near = []
        for s in range(SPECIES):
            sides = []
            if c > 0:
                sides.append(e[s, (c - 1) * 128 : c * 128])
            if c < 3:
                sides.append(e[s, (c + 1) * 128 : (c + 2) * 128])
            near.append(sides[0] + sides[1] if len(sides) == 2 else sides[0])
        for s, value in enumerate(local_rhs(u, near, ag[rows], deg[rows], ENDO_GAP)):
            stack(stacked, s, rows, value)
    c_we.wait()
    c_te.wait()
    finish(we, te, be, pge)
    outs.append(start(be, be_h))
    for s in range(SPECIES):
        pge[SLOTS : SLOTS + 128, col(s)] = be[s, 0:128]
        pge[SLOTS + 128 : SLOTS + 256, col(s)] = be[s, 384:512]
    outs.append(start(pge, pge_h))
    c_m.wait()
    c_sm.wait()
    if not first:
        c_zm.wait()
    advance(m, zm, sm)
    place = lax.broadcasted_iota(jnp.int32, (64, POINTS), 0)
    for c in range(8):
        rows = slice(c * 64, (c + 1) * 64)
        u = [m[s, rows] for s in range(SPECIES)]
        near = [
            jnp.where(place == 0, 0.0, pltpu.roll(x, 1, 0))
            + jnp.where(place == 63, 0.0, pltpu.roll(x, 63, 0))
            for x in u
        ]
        for s, value in enumerate(local_rhs(u, near, None, deg[rows], MUSCLE_GAP)):
            stack(stacked, s, rows, value)
    c_wm.wait()
    c_tm.wait()
    finish(wm, tm, bm, pgm)
    outs.append(start(bm, bm_h))
    for s in range(SPECIES):
        for c in range(8):
            first_row = bm[s, c * 64 : c * 64 + 1]
            last_row = bm[s, c * 64 + 63 : c * 64 + 64]
            pgm[SLOTS + c : SLOTS + c + 1, col(s)] = first_row
            pgm[SLOTS + 8 + c : SLOTS + 9 + c, col(s)] = last_row
    outs.append(start(pgm, pgm_h))
    for copy in outs:
        copy.wait()


def f32(*shape):
    return jax.ShapeDtypeStruct(shape, jnp.float32)


def bf16(*shape):
    return jax.ShapeDtypeStruct(shape, jnp.bfloat16)


def call(kernel, name, args, outs, scratch, flops, moved):
    far = pl.BlockSpec(memory_space=pl.ANY)
    return pl.pallas_call(
        kernel,
        out_shape=outs,
        in_specs=[far] * len(args),
        out_specs=[far] * len(outs),
        scratch_shapes=[pltpu.VMEM(a.shape, a.dtype) for a in scratch]
        + [pltpu.SemaphoreType.DMA((24,))],
        compiler_params=pltpu.CompilerParams(vmem_limit_bytes=VMEM_LIMIT),
        cost_estimate=pl.CostEstimate(flops=flops, bytes_accessed=moved, transcendentals=0),
        name=name,
    )(*args)


FIELD = f32(SPECIES, CELLS, POINTS)
LINEAR = f32(OWNERS * BLOCKS, POINTS)
ENDO_PARTS = bf16(ENDO_SLOTS, 2 * WIDE)
MUSCLE_PARTS = bf16(MUSCLE_SLOTS, 2 * WIDE)
ENDO_PICKED = f32(ENDO_SLOTS, WIDE)
MUSCLE_PICKED = f32(SLOTS + 16, WIDE)
STACKED = bf16(SPECIES, CELLS, 2 * POINTS)
ENDO_STACK = bf16(SPECIES, ENDO_SLOTS, 2 * POINTS)
MUSCLE_STACK = bf16(SPECIES, MUSCLE_SLOTS, 2 * POINTS)
CELL_PARTS = bf16(CELLS, 2 * WIDE)
ENDO_END = f32(SPECIES, 128, POINTS)
MUSCLE_END = f32(SPECIES, 8, POINTS)


def first_call(*args):
    return call(
        first_kernel, "first_rows", args, [LINEAR], [*args, CELL_PARTS, LINEAR],
        10**9, 3 * 10**6,
    )[0]


def post_call(*args):
    outs = [LINEAR, ENDO_PARTS, MUSCLE_PARTS, ENDO_END, ENDO_END, MUSCLE_END, MUSCLE_END]
    return call(
        post_kernel, "post", args, outs, [*args, *outs, ENDO_STACK, MUSCLE_STACK],
        10**9, 5 * 10**6,
    )


def last_call(*args):
    return call(
        last_kernel, "last_step", args, [FIELD, FIELD],
        [*args, ENDO_PARTS, MUSCLE_PARTS, ENDO_STACK, MUSCLE_STACK], 10**9, 5 * 10**6,
    )


def local_call(first, *args):
    outs = [FIELD, FIELD, ENDO_PICKED, MUSCLE_PICKED]
    rest = args[2:] if first else args[4:]
    return call(
        functools.partial(local_kernel, first), "local_part", args, outs,
        [FIELD, FIELD, ENDO_PARTS, MUSCLE_PARTS, *rest, *outs, STACKED, CELL_PARTS,
         f32(CELLS, POINTS)],
        2 * 10**9, 8 * 10**6,
    )


def weights(inverse):
    turned = inverse.transpose(0, 2, 1)
    rounded = lax.reduce_precision(turned, 8, 7)
    hi = rounded.astype(jnp.bfloat16)
    lo = (turned - rounded).astype(jnp.bfloat16)
    row = jnp.concatenate([hi, lo], axis=2)
    return jnp.concatenate([row, row], axis=1)


def one_hot(index, ends, slots):
    flat = index.T.reshape(-1)
    pad = jnp.full((slots - SLOTS - ends.size,), -1, jnp.int32)
    joined = jnp.concatenate([flat, ends, pad])
    cells = jnp.arange(CELLS, dtype=jnp.int32)
    spread = (cells[:, None] == joined[None, :]).astype(jnp.bfloat16)
    pick = (flat[:, None] == cells[None, :]).astype(jnp.bfloat16)
    wanted = jnp.concatenate([jnp.where(flat < 0, -2, flat), ends])
    passed = (wanted[:, None] == joined[None, :]).astype(jnp.bfloat16)
    return spread, pick, passed


def around(x, axis, step, closed):
    count = lax.axis_size(axis)
    pairs = [
        (i, (i + step) % count) for i in range(count) if closed or 0 <= i + step < count
    ]
    return lax.ppermute(x, axis, pairs)


def exchange(linear):
    out = lax.all_to_all(
        linear.reshape(OWNERS, BLOCKS // 2, 2, POINTS), DEVICES, split_axis=0, concat_axis=0,
        tiled=True,
    )
    return out.reshape(OWNERS * BLOCKS, POINTS)


def local(
    endothelium, muscle, agonist, proj_cell, proj_target, proj_count, endo_inverse, muscle_inverse
):
    e = endothelium.reshape(SPECIES, CELLS, POINTS)
    m = muscle.reshape(SPECIES, CELLS, POINTS)
    ag = agonist.reshape(CELLS, POINTS)
    slot_ids = jnp.arange(PAIR, dtype=jnp.int32)
    live = slot_ids[None, :] < proj_count[0][:, None]
    arrived = lax.all_to_all(
        jnp.where(live, proj_target[0], -1), DEVICES, split_axis=0, concat_axis=0, tiled=True
    )
    line = jnp.arange(128, dtype=jnp.int32)
    starts = jnp.arange(8, dtype=jnp.int32) * 64
    se, te, pe = one_hot(
        jnp.where(live, proj_cell[0], -1), jnp.concatenate([line, line + 384]), ENDO_SLOTS
    )
    sm, tm, pm = one_hot(arrived, jnp.concatenate([starts, starts + 63]), MUSCLE_SLOTS)
    we = weights(endo_inverse)
    wm = weights(muscle_inverse)
    e_top, e_bot = endothelium[:, 0], endothelium[:, 3]
    m_lo, m_hi = muscle[:, :, 0], muscle[:, :, 63]
    send = first_call(e, m, te, tm)
    state = (e, m)
    for step in range(TIME_STEPS):
        recv = exchange(send)
        halo = (
            around(e_bot, "ax", 1, False),
            around(e_top, "ax", -1, False),
            around(m_hi, "circ", 1, True),
            around(m_lo, "circ", -1, True),
        )
        be, bm, pge, pgm = local_call(step == 0, *state, ag, se, sm, te, tm, we, wm)
        if step < TIME_STEPS - 1:
            send, ze, zm, e_top, e_bot, m_lo, m_hi = post_call(
                recv, *halo, we, wm, pe, pm, pge, pgm
            )
            state = (be, bm, ze, zm)
        else:
            e, m = last_call(recv, *halo, we, wm, se, sm, be, bm)
    return e.reshape(endothelium.shape), m.reshape(muscle.shape)


def solution(mesh):
    placed = (
        P(None, "ax", "circ", None),
        P(None, "ax", "circ", None),
        P("ax", "circ", None),
        P(("ax", "circ"), None, None),
        P(("ax", "circ"), None, None),
        P(("ax", "circ"), None),
        P(),
        P(),
    )
    return jax.shard_map(
        local,
        mesh=mesh,
        in_specs=placed,
        out_specs=(P(None, "ax", "circ", None), P(None, "ax", "circ", None)),
        check_vma=False,
    )
```

```python
import functools

import jax
import jax.numpy as jnp
from jax import lax
from jax.experimental import pallas as pl
from jax.experimental.pallas import tpu as pltpu
from jax.sharding import PartitionSpec as P

TIME_STEPS = 8
TIME_STEP = 0.2
COUPLING = (0.1, 0.3, 0.5)
ENDO_GAP = (0.05, 0.3, 0.5)
MUSCLE_GAP = (0.05, 0.1, 0.4)
DEVICES = ("ax", "circ")
PAIR = 2
SPECIES = 3
POINTS = 128
CELLS = 512
OWNERS = 128
HALF = SPECIES * PAIR
BLOCKS = 2 * HALF
SLOTS = PAIR * OWNERS
ENDO_SLOTS = SLOTS + 256
MUSCLE_SLOTS = SLOTS + 128
WIDE = SPECIES * POINTS
VMEM_LIMIT = 48 * 1024 * 1024
ENDO_BASE = 0
MUSCLE_BASE = ENDO_BASE + SPECIES * CELLS
PICKS = MUSCLE_BASE + SPECIES * CELLS
ENDO_GAIN = PICKS + 2 * SPECIES * SLOTS
MUSCLE_GAIN = ENDO_GAIN + SPECIES * ENDO_SLOTS
MUSCLE_ENDS = MUSCLE_GAIN + SPECIES * (SLOTS + 16)
STORE_ROWS = 34816


def col(i):
    return slice(i * POINTS, (i + 1) * POINTS)


def halves(x):
    hi = x.astype(jnp.bfloat16)
    lo = (x - hi.astype(jnp.float32)).astype(jnp.bfloat16)
    return hi, lo


def dot(a, b):
    return jnp.dot(a, b, preferred_element_type=jnp.float32)


def store_parts(parts, s, rows, value):
    hi, lo = halves(value)
    parts[rows, col(s)] = hi
    parts[rows, col(SPECIES + s)] = lo


def both(wide, s):
    return wide[:, col(s)] + wide[:, col(SPECIES + s)]


def slot_rows(base, s, k):
    return pl.ds(base + s * PAIR + k, OWNERS, stride=BLOCKS)


def local_rhs(u, near, drive, deg, gaps):
    decay = (0.6, 0.5, 0.8)
    square = u[1] * u[1]
    release = square / (0.5 + square)
    own = [
        u[s]
        * ((1.0 - TIME_STEP * (decay[s] + 2.0 * gaps[s])) - (TIME_STEP * COUPLING[s]) * deg)
        + (TIME_STEP * gaps[s]) * near[s]
        for s in range(SPECIES)
    ]
    own[0] = own[0] + (TIME_STEP * 1.2) * release - (TIME_STEP * 0.2) * u[2]
    if drive is not None:
        own[1] = own[1] + TIME_STEP * drive
    own[2] = own[2] + (TIME_STEP * 0.5) * u[0]
    return own


def stack(stacked, s, rows, value):
    hi, lo = halves(value)
    stacked[s, rows, 0:POINTS] = hi
    stacked[s, rows, POINTS:] = lo


def mover(sems):
    used = []

    def start(source, dest):
        copy = pltpu.make_async_copy(source, dest, sems.at[len(used)])
        used.append(copy)
        copy.start()
        return copy

    return start


def through(stacked, weight, gaps, parts, gain, count):
    for s in range(SPECIES):
        wide = dot(stacked[s], weight[s])
        value = wide[:, :POINTS] + wide[:, POINTS:]
        slots = value[:SLOTS] * (TIME_STEP * COUPLING[s])
        halo = value[SLOTS:] * (TIME_STEP * gaps[s])
        store_parts(parts, s, slice(0, SLOTS), slots)
        store_parts(parts, s, slice(SLOTS, parts.shape[0]), halo)
        gain[s * count : s * count + SLOTS] = slots
        gain[s * count + SLOTS : (s + 1) * count] = halo[: count - SLOTS]


def endo_slots(recv, eu, ed, stacked):
    for s in range(SPECIES):
        for k in range(PAIR):
            rows = slice(k * OWNERS, (k + 1) * OWNERS)
            stack(stacked, s, rows, recv[slot_rows(HALF, s, k), :])
        stack(stacked, s, slice(SLOTS, SLOTS + 128), eu[s])
        stack(stacked, s, slice(SLOTS + 128, SLOTS + 256), ed[s])


def muscle_slots(recv, ml, mr, stacked):
    for s in range(SPECIES):
        for k in range(PAIR):
            rows = slice(k * OWNERS, (k + 1) * OWNERS)
            stack(stacked, s, rows, recv[slot_rows(0, s, k), :])
        both_ends = jnp.concatenate([ml[s], mr[s]], axis=0)
        stack(stacked, s, slice(SLOTS, SLOTS + 16), both_ends)
        stacked[s, SLOTS + 16 : MUSCLE_SLOTS, :] = jnp.zeros(
            (MUSCLE_SLOTS - SLOTS - 16, 2 * POINTS), jnp.bfloat16
        )


def first_kernel(e_h, m_h, te_h, tm_h, send_h, e, m, te, tm, parts, send, sems):
    start = mover(sems)
    into = [start(a, b) for a, b in ((e_h, e), (te_h, te), (m_h, m), (tm_h, tm))]
    for field, pick, base, ready in ((e, te, 0, into[:2]), (m, tm, HALF, into[2:])):
        for copy in ready:
            copy.wait()
        for s in range(SPECIES):
            store_parts(parts, s, slice(None), field[s])
        rows = dot(pick[...], parts[...])
        for s in range(SPECIES):
            value = both(rows, s)
            for k in range(PAIR):
                send[slot_rows(base, s, k), :] = value[k * OWNERS : (k + 1) * OWNERS]
    start(send, send_h).wait()


def add_endo(field, gain, spread, parts):
    for s in range(SPECIES):
        store_parts(parts, s, slice(None), gain[s * ENDO_SLOTS : s * ENDO_SLOTS + SLOTS])
    total = dot(spread[...], parts[...])
    for s in range(SPECIES):
        at = s * ENDO_SLOTS + SLOTS
        value = both(total, s)
        field[s * CELLS : s * CELLS + 128] += value[0:128] + gain[at : at + 128]
        field[s * CELLS + 128 : s * CELLS + 384] += value[128:384]
        field[s * CELLS + 384 : (s + 1) * CELLS] += value[384:] + gain[at + 128 : at + 256]


def add_muscle(field, gain, spread, parts):
    count = SLOTS + 16
    for s in range(SPECIES):
        store_parts(parts, s, slice(None), gain[s * count : s * count + SLOTS])
    total = dot(spread[...], parts[...])
    for s in range(SPECIES):
        field[s * CELLS : (s + 1) * CELLS] += both(total, s)
        for c in range(8):
            low, high = s * CELLS + c * 64, s * CELLS + c * 64 + 63
            at = s * count + SLOTS + c
            field[low : low + 1] += gain[at : at + 1]
            field[high : high + 1] += gain[at + 8 : at + 9]


def post_kernel(
    recv_h, eu, ed, ml, mr, we, wm, pe, pm, store_in,
    send_h, et, eb, mlo, mhi, store,
    recv, picks, ends, muscle_ends, send, ze, zm, gain_e, gain_m, stacked_e, stacked_m, sems,
):
    start = mover(sems)
    c_recv = start(recv_h, recv)
    c_picks = start(store_in.at[PICKS : PICKS + 2 * SPECIES * SLOTS], picks)
    into = [start(store_in.at[MUSCLE_ENDS : MUSCLE_ENDS + 48], muscle_ends)]
    for s in range(SPECIES):
        for k, at in enumerate((0, 384)):
            row = ENDO_BASE + s * CELLS + at
            dest = (s * 2 + k) * 128
            into.append(start(store_in.at[row : row + 128], ends.at[dest : dest + 128]))
    outs = []
    c_recv.wait()
    endo_slots(recv, eu, ed, stacked_e)
    through(stacked_e, we, ENDO_GAP, ze, gain_e, ENDO_SLOTS)
    outs.append(start(gain_e, store.at[ENDO_GAIN : ENDO_GAIN + SPECIES * ENDO_SLOTS]))
    rows = dot(pe[0:SLOTS], ze[...])
    c_picks.wait()
    for s in range(SPECIES):
        value = both(rows, s) + picks[s * SLOTS : (s + 1) * SLOTS]
        for k in range(PAIR):
            send[slot_rows(0, s, k), :] = value[k * OWNERS : (k + 1) * OWNERS]
    muscle_slots(recv, ml, mr, stacked_m)
    through(stacked_m, wm, MUSCLE_GAP, zm, gain_m, SLOTS + 16)
    outs.append(start(gain_m, store.at[MUSCLE_GAIN : MUSCLE_GAIN + SPECIES * (SLOTS + 16)]))
    rows = dot(pm[...], zm[...])
    for copy in into:
        copy.wait()
    for s in range(SPECIES):
        value = both(rows, s)
        moved = value[:SLOTS] + picks[(SPECIES + s) * SLOTS : (SPECIES + s + 1) * SLOTS]
        for k in range(PAIR):
            send[slot_rows(HALF, s, k), :] = moved[k * OWNERS : (k + 1) * OWNERS]
        edge = value[SLOTS : SLOTS + 16] + muscle_ends[s * 16 : (s + 1) * 16]
        mlo[s] = edge[0:8]
        mhi[s] = edge[8:16]
    outs.append(start(send, send_h))
    rows = dot(pe[SLOTS:], ze[...])
    for s in range(SPECIES):
        value = both(rows, s)
        et[s] = value[:128] + ends[s * 256 : s * 256 + 128]
        eb[s] = value[128:] + ends[s * 256 + 128 : s * 256 + 256]
    for copy in outs:
        copy.wait()


def last_kernel(
    recv, eu, ed, ml, mr, we, wm, se, sm, store,
    e_h, m_h,
    e, m, ze, zm, gain_e, gain_m, parts, stacked_e, stacked_m, sems,
):
    start = mover(sems)
    c_e = start(store.at[ENDO_BASE : ENDO_BASE + SPECIES * CELLS], e)
    c_m = start(store.at[MUSCLE_BASE : MUSCLE_BASE + SPECIES * CELLS], m)
    endo_slots(recv, eu, ed, stacked_e)
    through(stacked_e, we, ENDO_GAP, ze, gain_e, ENDO_SLOTS)
    c_e.wait()
    add_endo(e, gain_e, se, parts)
    out_e = start(e, e_h)
    muscle_slots(recv, ml, mr, stacked_m)
    through(stacked_m, wm, MUSCLE_GAP, zm, gain_m, SLOTS + 16)
    c_m.wait()
    add_muscle(m, gain_m, sm, parts)
    out_m = start(m, m_h)
    out_e.wait()
    out_m.wait()


def local_kernel(first, *refs):
    start = mover(refs[-1])
    (ag, se, sm, te, tm, we, wm), refs = refs[:7], refs[7:-1]
    if first:
        (e_h, m_h, store, *refs) = refs
    else:
        (store_in, store, *refs) = refs
        e_h = store_in.at[ENDO_BASE : ENDO_BASE + SPECIES * CELLS]
        m_h = store_in.at[MUSCLE_BASE : MUSCLE_BASE + SPECIES * CELLS]
    e, m, gain_e, gain_m, be, bm, picks, muscle_ends, stacked, parts, slot_parts, deg = refs
    c_e = start(e_h, e)
    if not first:
        c_ge = start(store_in.at[ENDO_GAIN : ENDO_GAIN + SPECIES * ENDO_SLOTS], gain_e)
    c_m = start(m_h, m)
    if not first:
        c_gm = start(store_in.at[MUSCLE_GAIN : MUSCLE_GAIN + SPECIES * (SLOTS + 16)], gain_m)
    ones = jnp.ones((SLOTS, POINTS), jnp.bfloat16)
    outs = []

    def finish(weight, pick, base, at):
        for s in range(SPECIES):
            wide = dot(stacked[s], weight[s])
            value = wide[:, :POINTS] + wide[:, POINTS:]
            base[s * CELLS : (s + 1) * CELLS] = value
            store_parts(parts, s, slice(None), value)
        rows = dot(pick[...], parts[...])
        for s in range(SPECIES):
            picks[at + s * SLOTS : at + (s + 1) * SLOTS] = both(rows, s)

    deg[...] = dot(se[...], ones)
    c_e.wait()
    if not first:
        c_ge.wait()
        add_endo(e, gain_e, se, slot_parts)
    for c in range(4):
        rows = slice(c * 128, (c + 1) * 128)
        u = [e[s * CELLS + c * 128 : s * CELLS + (c + 1) * 128] for s in range(SPECIES)]
        near = []
        for s in range(SPECIES):
            at = s * CELLS + c * 128
            sides = []
            if c > 0:
                sides.append(e[at - 128 : at])
            if c < 3:
                sides.append(e[at + 128 : at + 256])
            near.append(sides[0] + sides[1] if len(sides) == 2 else sides[0])
        for s, value in enumerate(local_rhs(u, near, ag[rows], deg[rows], ENDO_GAP)):
            stack(stacked, s, rows, value)
    finish(we, te, be, 0)
    outs.append(start(be, store.at[ENDO_BASE : ENDO_BASE + SPECIES * CELLS]))
    deg[...] = dot(sm[...], ones)
    c_m.wait()
    if not first:
        c_gm.wait()
        add_muscle(m, gain_m, sm, slot_parts)
    place = lax.broadcasted_iota(jnp.int32, (64, POINTS), 0)
    for c in range(8):
        rows = slice(c * 64, (c + 1) * 64)
        u = [m[s * CELLS + c * 64 : s * CELLS + (c + 1) * 64] for s in range(SPECIES)]
        near = [
            jnp.where(place == 0, 0.0, pltpu.roll(x, 1, 0))
            + jnp.where(place == 63, 0.0, pltpu.roll(x, 63, 0))
            for x in u
        ]
        for s, value in enumerate(local_rhs(u, near, None, deg[rows], MUSCLE_GAP)):
            stack(stacked, s, rows, value)
    finish(wm, tm, bm, SPECIES * SLOTS)
    outs.append(start(bm, store.at[MUSCLE_BASE : MUSCLE_BASE + SPECIES * CELLS]))
    outs.append(start(picks, store.at[PICKS : PICKS + 2 * SPECIES * SLOTS]))
    for s in range(SPECIES):
        for c in range(8):
            low, high = s * CELLS + c * 64, s * CELLS + c * 64 + 63
            muscle_ends[s * 16 + c : s * 16 + c + 1] = bm[low : low + 1]
            muscle_ends[s * 16 + 8 + c : s * 16 + 9 + c] = bm[high : high + 1]
    outs.append(start(muscle_ends, store.at[MUSCLE_ENDS : MUSCLE_ENDS + 48]))
    for copy in outs:
        copy.wait()


def f32(*shape):
    return jax.ShapeDtypeStruct(shape, jnp.float32)


def bf16(*shape):
    return jax.ShapeDtypeStruct(shape, jnp.bfloat16)


def call(kernel, name, args, far_in, outs, far_out, scratch, flops, moved, aliases):
    far = pl.BlockSpec(memory_space=pl.ANY)
    near = pl.BlockSpec(memory_space=pltpu.VMEM)
    return pl.pallas_call(
        kernel,
        out_shape=outs,
        in_specs=[far if i in far_in else near for i in range(len(args))],
        out_specs=[far if i in far_out else near for i in range(len(outs))],
        scratch_shapes=[pltpu.VMEM(a.shape, a.dtype) for a in scratch]
        + [pltpu.SemaphoreType.DMA((24,))],
        compiler_params=pltpu.CompilerParams(vmem_limit_bytes=VMEM_LIMIT),
        cost_estimate=pl.CostEstimate(flops=flops, bytes_accessed=moved, transcendentals=0),
        input_output_aliases=aliases,
        name=name,
    )(*args)


FIELD = f32(SPECIES * CELLS, POINTS)
LINEAR = f32(OWNERS * BLOCKS, POINTS)
STORE = f32(STORE_ROWS, POINTS)
ENDO_PARTS = bf16(ENDO_SLOTS, 2 * WIDE)
MUSCLE_PARTS = bf16(MUSCLE_SLOTS, 2 * WIDE)
SLOT_PARTS = bf16(SLOTS, 2 * WIDE)
ENDO_GAINS = f32(SPECIES * ENDO_SLOTS, POINTS)
MUSCLE_GAINS = f32(SPECIES * (SLOTS + 16), POINTS)
PICKED = f32(2 * SPECIES * SLOTS, POINTS)
EDGES = f32(SPECIES * 16, POINTS)
STACKED = bf16(SPECIES, CELLS, 2 * POINTS)
ENDO_STACK = bf16(SPECIES, ENDO_SLOTS, 2 * POINTS)
MUSCLE_STACK = bf16(SPECIES, MUSCLE_SLOTS, 2 * POINTS)
CELL_PARTS = bf16(CELLS, 2 * WIDE)
ENDO_END = f32(SPECIES, 128, POINTS)
MUSCLE_END = f32(SPECIES, 8, POINTS)
SLOT_SCRATCH = [ENDO_PARTS, MUSCLE_PARTS, ENDO_GAINS, MUSCLE_GAINS]


def first_call(*args):
    field = f32(SPECIES, CELLS, POINTS)
    pick = bf16(SLOTS, CELLS)
    return call(
        first_kernel, "first_rows", args, range(4), [LINEAR], range(1),
        [field, field, pick, pick, CELL_PARTS, LINEAR], 10**9, 3 * 10**6, {},
    )[0]


def post_call(*args):
    outs = [LINEAR, ENDO_END, ENDO_END, MUSCLE_END, MUSCLE_END, STORE]
    return call(
        post_kernel, "post", args, (0, 9), outs, (0, 5),
        [LINEAR, PICKED, f32(SPECIES * 256, POINTS), EDGES, LINEAR, *SLOT_SCRATCH, ENDO_STACK,
         MUSCLE_STACK],
        10**9, 5 * 10**6, {0: 0, 9: 5},
    )


def last_call(*args):
    return call(
        last_kernel, "last_step", args, (9,), [FIELD, FIELD], (0, 1),
        [FIELD, FIELD, *SLOT_SCRATCH, SLOT_PARTS, ENDO_STACK, MUSCLE_STACK],
        10**9, 5 * 10**6, {},
    )


def local_call(first, *args):
    return call(
        functools.partial(local_kernel, first), "local_part", args, (7, 8), [STORE], (0,),
        [FIELD, FIELD, ENDO_GAINS, MUSCLE_GAINS, FIELD, FIELD, PICKED, EDGES, STACKED,
         CELL_PARTS, SLOT_PARTS, f32(CELLS, POINTS)],
        2 * 10**9, 8 * 10**6, {} if first else {7: 0},
    )[0]


def weights(inverse):
    turned = inverse.transpose(0, 2, 1)
    rounded = lax.reduce_precision(turned, 8, 7)
    hi = rounded.astype(jnp.bfloat16)
    lo = (turned - rounded).astype(jnp.bfloat16)
    row = jnp.concatenate([hi, lo], axis=2)
    return jnp.concatenate([row, row], axis=1)


def one_hot(index, ends, slots):
    flat = index.T.reshape(-1)
    pad = jnp.full((slots - SLOTS - ends.size,), -1, jnp.int32)
    joined = jnp.concatenate([flat, ends, pad])
    cells = jnp.arange(CELLS, dtype=jnp.int32)
    spread = (cells[:, None] == flat[None, :]).astype(jnp.bfloat16)
    pick = (flat[:, None] == cells[None, :]).astype(jnp.bfloat16)
    wanted = jnp.concatenate([jnp.where(flat < 0, -2, flat), ends])
    passed = (wanted[:, None] == joined[None, :]).astype(jnp.bfloat16)
    return spread, pick, passed


def around(x, axis, step, closed):
    count = lax.axis_size(axis)
    pairs = [
        (i, (i + step) % count) for i in range(count) if closed or 0 <= i + step < count
    ]
    return lax.ppermute(x, axis, pairs)


def exchange(linear):
    out = lax.all_to_all(
        linear.reshape(OWNERS, BLOCKS // 2, 2, POINTS), DEVICES, split_axis=0, concat_axis=0,
        tiled=True,
    )
    return out.reshape(OWNERS * BLOCKS, POINTS)


def local(
    endothelium, muscle, agonist, proj_cell, proj_target, proj_count, endo_inverse, muscle_inverse
):
    e = endothelium.reshape(SPECIES, CELLS, POINTS)
    m = muscle.reshape(SPECIES, CELLS, POINTS)
    ag = agonist.reshape(CELLS, POINTS)
    slot_ids = jnp.arange(PAIR, dtype=jnp.int32)
    live = slot_ids[None, :] < proj_count[0][:, None]
    arrived = lax.all_to_all(
        jnp.where(live, proj_target[0], -1), DEVICES, split_axis=0, concat_axis=0, tiled=True
    )
    line = jnp.arange(128, dtype=jnp.int32)
    starts = jnp.arange(8, dtype=jnp.int32) * 64
    se, te, pe = one_hot(
        jnp.where(live, proj_cell[0], -1), jnp.concatenate([line, line + 384]), ENDO_SLOTS
    )
    sm, tm, pm = one_hot(arrived, jnp.concatenate([starts, starts + 63]), MUSCLE_SLOTS)
    we = weights(endo_inverse)
    wm = weights(muscle_inverse)
    e_top, e_bot = endothelium[:, 0], endothelium[:, 3]
    m_lo, m_hi = muscle[:, :, 0], muscle[:, :, 63]
    send = first_call(e, m, te, tm)
    store = None
    for step in range(TIME_STEPS):
        recv = exchange(send)
        halo = (
            around(e_bot, "ax", 1, False),
            around(e_top, "ax", -1, False),
            around(m_hi, "circ", 1, True),
            around(m_lo, "circ", -1, True),
        )
        state = (e.reshape(FIELD.shape), m.reshape(FIELD.shape)) if step == 0 else (store,)
        store = local_call(step == 0, ag, se, sm, te, tm, we, wm, *state)
        if step < TIME_STEPS - 1:
            send, e_top, e_bot, m_lo, m_hi, store = post_call(
                recv, *halo, we, wm, pe, pm, store
            )
        else:
            e, m = last_call(recv, *halo, we, wm, se, sm, store)
    return e.reshape(endothelium.shape), m.reshape(muscle.shape)


def solution(mesh):
    placed = (
        P(None, "ax", "circ", None),
        P(None, "ax", "circ", None),
        P("ax", "circ", None),
        P(("ax", "circ"), None, None),
        P(("ax", "circ"), None, None),
        P(("ax", "circ"), None),
        P(),
        P(),
    )
    return jax.shard_map(
        local,
        mesh=mesh,
        in_specs=placed,
        out_specs=(P(None, "ax", "circ", None), P(None, "ax", "circ", None)),
        check_vma=False,
    )
```

```python
import functools

import jax
import jax.numpy as jnp
from jax import lax
from jax.experimental import pallas as pl
from jax.experimental.pallas import tpu as pltpu
from jax.sharding import PartitionSpec as P

TIME_STEPS = 8
TIME_STEP = 0.2
COUPLING = (0.1, 0.3, 0.5)
ENDO_GAP = (0.05, 0.3, 0.5)
MUSCLE_GAP = (0.05, 0.1, 0.4)
DEVICES = ("ax", "circ")
PAIR = 2
SPECIES = 3
POINTS = 128
CELLS = 512
OWNERS = 128
HALF = SPECIES * PAIR
BLOCKS = 2 * HALF
SLOTS = PAIR * OWNERS
ENDO_SLOTS = SLOTS + 256
MUSCLE_SLOTS = SLOTS + 128
WIDE = SPECIES * POINTS
VMEM_LIMIT = 48 * 1024 * 1024
ENDO_BASE = 0
MUSCLE_BASE = ENDO_BASE + SPECIES * CELLS
PICKS = MUSCLE_BASE + SPECIES * CELLS
ENDO_GAIN = PICKS + 2 * SPECIES * SLOTS
MUSCLE_GAIN = ENDO_GAIN + SPECIES * ENDO_SLOTS
MUSCLE_ENDS = MUSCLE_GAIN + SPECIES * (SLOTS + 16)
STORE_ROWS = 34816


def col(i):
    return slice(i * POINTS, (i + 1) * POINTS)


def halves(x):
    hi = x.astype(jnp.bfloat16)
    lo = (x - hi.astype(jnp.float32)).astype(jnp.bfloat16)
    return hi, lo


def dot(a, b):
    return jnp.dot(a, b, preferred_element_type=jnp.float32)


def store_parts(parts, s, rows, value):
    hi, lo = halves(value)
    parts[rows, col(s)] = hi
    parts[rows, col(SPECIES + s)] = lo


def both(wide, s):
    return wide[:, col(s)] + wide[:, col(SPECIES + s)]


def slot_rows(base, s, k):
    return pl.ds(base + s * PAIR + k, OWNERS, stride=BLOCKS)


def local_rhs(u, near, drive, deg, gaps):
    decay = (0.6, 0.5, 0.8)
    square = u[1] * u[1]
    release = square / (0.5 + square)
    own = [
        u[s]
        * ((1.0 - TIME_STEP * (decay[s] + 2.0 * gaps[s])) - (TIME_STEP * COUPLING[s]) * deg)
        + (TIME_STEP * gaps[s]) * near[s]
        for s in range(SPECIES)
    ]
    own[0] = own[0] + (TIME_STEP * 1.2) * release - (TIME_STEP * 0.2) * u[2]
    if drive is not None:
        own[1] = own[1] + TIME_STEP * drive
    own[2] = own[2] + (TIME_STEP * 0.5) * u[0]
    return own


def stack(stacked, s, rows, value):
    hi, lo = halves(value)
    stacked[s, rows, 0:POINTS] = hi
    stacked[s, rows, POINTS:] = lo


def mover(sems):
    used = []

    def start(source, dest):
        copy = pltpu.make_async_copy(source, dest, sems.at[len(used)])
        used.append(copy)
        copy.start()
        return copy

    return start


def through(stacked, weight, gaps, parts, gain, count):
    for s in range(SPECIES):
        wide = dot(stacked[s], weight[s])
        value = wide[:, :POINTS] + wide[:, POINTS:]
        slots = value[:SLOTS] * (TIME_STEP * COUPLING[s])
        halo = value[SLOTS:] * (TIME_STEP * gaps[s])
        store_parts(parts, s, slice(0, SLOTS), slots)
        store_parts(parts, s, slice(SLOTS, parts.shape[0]), halo)
        gain[s * count : s * count + SLOTS] = slots
        gain[s * count + SLOTS : (s + 1) * count] = halo[: count - SLOTS]


def doubled(row, full):
    for s in range(SPECIES):
        full[s, 0:POINTS] = row[s]
        full[s, POINTS:] = row[s]


def split_inverse(inverse, row):
    for s in range(SPECIES):
        hi, lo = halves(inverse[s].T)
        row[s, :, 0:POINTS] = hi
        row[s, :, POINTS:] = lo


def endo_slots(recv, eu, ed, stacked):
    for s in range(SPECIES):
        for k in range(PAIR):
            rows = slice(k * OWNERS, (k + 1) * OWNERS)
            stack(stacked, s, rows, recv[slot_rows(HALF, s, k), :])
        stack(stacked, s, slice(SLOTS, SLOTS + 128), eu[s])
        stack(stacked, s, slice(SLOTS + 128, SLOTS + 256), ed[s])


def muscle_slots(recv, ml, mr, stacked):
    for s in range(SPECIES):
        for k in range(PAIR):
            rows = slice(k * OWNERS, (k + 1) * OWNERS)
            stack(stacked, s, rows, recv[slot_rows(0, s, k), :])
        both_ends = jnp.concatenate([ml[s], mr[s]], axis=0)
        stack(stacked, s, slice(SLOTS, SLOTS + 16), both_ends)
        stacked[s, SLOTS + 16 : MUSCLE_SLOTS, :] = jnp.zeros(
            (MUSCLE_SLOTS - SLOTS - 16, 2 * POINTS), jnp.bfloat16
        )


def first_kernel(e_h, m_h, te_h, tm_h, send_h, e, m, te, tm, parts, send, sems):
    start = mover(sems)
    into = [start(a, b) for a, b in ((e_h, e), (te_h, te), (m_h, m), (tm_h, tm))]
    for field, pick, base, ready in ((e, te, 0, into[:2]), (m, tm, HALF, into[2:])):
        for copy in ready:
            copy.wait()
        for s in range(SPECIES):
            store_parts(parts, s, slice(None), field[s])
        rows = dot(pick[...], parts[...])
        for s in range(SPECIES):
            value = both(rows, s)
            for k in range(PAIR):
                send[slot_rows(base, s, k), :] = value[k * OWNERS : (k + 1) * OWNERS]
    start(send, send_h).wait()


def add_endo(field, gain, spread, parts):
    for s in range(SPECIES):
        store_parts(parts, s, slice(None), gain[s * ENDO_SLOTS : s * ENDO_SLOTS + SLOTS])
    total = dot(spread[...], parts[...])
    for s in range(SPECIES):
        at = s * ENDO_SLOTS + SLOTS
        value = both(total, s)
        field[s * CELLS : s * CELLS + 128] += value[0:128] + gain[at : at + 128]
        field[s * CELLS + 128 : s * CELLS + 384] += value[128:384]
        field[s * CELLS + 384 : (s + 1) * CELLS] += value[384:] + gain[at + 128 : at + 256]


def add_muscle(field, gain, spread, parts):
    count = SLOTS + 16
    for s in range(SPECIES):
        store_parts(parts, s, slice(None), gain[s * count : s * count + SLOTS])
    total = dot(spread[...], parts[...])
    for s in range(SPECIES):
        field[s * CELLS : (s + 1) * CELLS] += both(total, s)
        for c in range(8):
            low, high = s * CELLS + c * 64, s * CELLS + c * 64 + 63
            at = s * count + SLOTS + c
            field[low : low + 1] += gain[at : at + 1]
            field[high : high + 1] += gain[at + 8 : at + 9]


def post_kernel(
    recv_h, eu, ed, ml, mr, we_row, wm_row, pe, pm, store_in,
    send_h, et, eb, mlo, mhi, store,
    recv, picks, ends, muscle_ends, send, ze, zm, gain_e, gain_m, stacked_e, stacked_m, we, wm,
    sems,
):
    start = mover(sems)
    c_recv = start(recv_h, recv)
    c_picks = start(store_in.at[PICKS : PICKS + 2 * SPECIES * SLOTS], picks)
    into = [start(store_in.at[MUSCLE_ENDS : MUSCLE_ENDS + 48], muscle_ends)]
    for s in range(SPECIES):
        for k, at in enumerate((0, 384)):
            row = ENDO_BASE + s * CELLS + at
            dest = (s * 2 + k) * 128
            into.append(start(store_in.at[row : row + 128], ends.at[dest : dest + 128]))
    outs = []
    doubled(we_row, we)
    doubled(wm_row, wm)
    c_recv.wait()
    endo_slots(recv, eu, ed, stacked_e)
    through(stacked_e, we, ENDO_GAP, ze, gain_e, ENDO_SLOTS)
    outs.append(start(gain_e, store.at[ENDO_GAIN : ENDO_GAIN + SPECIES * ENDO_SLOTS]))
    rows = dot(pe[0:SLOTS], ze[...])
    c_picks.wait()
    for s in range(SPECIES):
        value = both(rows, s) + picks[s * SLOTS : (s + 1) * SLOTS]
        for k in range(PAIR):
            send[slot_rows(0, s, k), :] = value[k * OWNERS : (k + 1) * OWNERS]
    muscle_slots(recv, ml, mr, stacked_m)
    through(stacked_m, wm, MUSCLE_GAP, zm, gain_m, SLOTS + 16)
    outs.append(start(gain_m, store.at[MUSCLE_GAIN : MUSCLE_GAIN + SPECIES * (SLOTS + 16)]))
    rows = dot(pm[...], zm[...])
    for copy in into:
        copy.wait()
    for s in range(SPECIES):
        value = both(rows, s)
        moved = value[:SLOTS] + picks[(SPECIES + s) * SLOTS : (SPECIES + s + 1) * SLOTS]
        for k in range(PAIR):
            send[slot_rows(HALF, s, k), :] = moved[k * OWNERS : (k + 1) * OWNERS]
        edge = value[SLOTS : SLOTS + 16] + muscle_ends[s * 16 : (s + 1) * 16]
        mlo[s] = edge[0:8]
        mhi[s] = edge[8:16]
    outs.append(start(send, send_h))
    rows = dot(pe[SLOTS:], ze[...])
    for s in range(SPECIES):
        value = both(rows, s)
        et[s] = value[:128] + ends[s * 256 : s * 256 + 128]
        eb[s] = value[128:] + ends[s * 256 + 128 : s * 256 + 256]
    for copy in outs:
        copy.wait()


def last_kernel(
    recv, eu, ed, ml, mr, we_row, wm_row, se, sm, store,
    e_h, m_h,
    e, m, ze, zm, gain_e, gain_m, parts, stacked_e, stacked_m, we, wm, sems,
):
    start = mover(sems)
    doubled(we_row, we)
    doubled(wm_row, wm)
    c_e = start(store.at[ENDO_BASE : ENDO_BASE + SPECIES * CELLS], e)
    c_m = start(store.at[MUSCLE_BASE : MUSCLE_BASE + SPECIES * CELLS], m)
    endo_slots(recv, eu, ed, stacked_e)
    through(stacked_e, we, ENDO_GAP, ze, gain_e, ENDO_SLOTS)
    c_e.wait()
    add_endo(e, gain_e, se, parts)
    out_e = start(e, e_h)
    muscle_slots(recv, ml, mr, stacked_m)
    through(stacked_m, wm, MUSCLE_GAP, zm, gain_m, SLOTS + 16)
    c_m.wait()
    add_muscle(m, gain_m, sm, parts)
    out_m = start(m, m_h)
    out_e.wait()
    out_m.wait()


def local_kernel(first, *refs):
    start = mover(refs[-1])
    (ag, se, sm, te, tm, we_row, wm_row), refs = refs[:7], refs[7:-1]
    if first:
        inverse_e, inverse_m = we_row, wm_row
        (e_h, m_h, store, we_row, wm_row, *refs) = refs
    else:
        (store_in, store, *refs) = refs
        e_h = store_in.at[ENDO_BASE : ENDO_BASE + SPECIES * CELLS]
        m_h = store_in.at[MUSCLE_BASE : MUSCLE_BASE + SPECIES * CELLS]
    (e, m, gain_e, gain_m, be, bm, picks, muscle_ends, stacked, parts, slot_parts, deg,
     we, wm) = refs
    c_e = start(e_h, e)
    if not first:
        c_ge = start(store_in.at[ENDO_GAIN : ENDO_GAIN + SPECIES * ENDO_SLOTS], gain_e)
    c_m = start(m_h, m)
    if not first:
        c_gm = start(store_in.at[MUSCLE_GAIN : MUSCLE_GAIN + SPECIES * (SLOTS + 16)], gain_m)
    if first:
        split_inverse(inverse_e, we_row)
        split_inverse(inverse_m, wm_row)
    doubled(we_row, we)
    doubled(wm_row, wm)
    ones = jnp.ones((SLOTS, POINTS), jnp.bfloat16)
    outs = []

    def finish(weight, pick, base, at):
        for s in range(SPECIES):
            wide = dot(stacked[s], weight[s])
            value = wide[:, :POINTS] + wide[:, POINTS:]
            base[s * CELLS : (s + 1) * CELLS] = value
            store_parts(parts, s, slice(None), value)
        rows = dot(pick[...], parts[...])
        for s in range(SPECIES):
            picks[at + s * SLOTS : at + (s + 1) * SLOTS] = both(rows, s)

    deg[...] = dot(se[...], ones)
    c_e.wait()
    if not first:
        c_ge.wait()
        add_endo(e, gain_e, se, slot_parts)
    for c in range(4):
        rows = slice(c * 128, (c + 1) * 128)
        u = [e[s * CELLS + c * 128 : s * CELLS + (c + 1) * 128] for s in range(SPECIES)]
        near = []
        for s in range(SPECIES):
            at = s * CELLS + c * 128
            sides = []
            if c > 0:
                sides.append(e[at - 128 : at])
            if c < 3:
                sides.append(e[at + 128 : at + 256])
            near.append(sides[0] + sides[1] if len(sides) == 2 else sides[0])
        for s, value in enumerate(local_rhs(u, near, ag[rows], deg[rows], ENDO_GAP)):
            stack(stacked, s, rows, value)
    finish(we, te, be, 0)
    outs.append(start(be, store.at[ENDO_BASE : ENDO_BASE + SPECIES * CELLS]))
    deg[...] = dot(sm[...], ones)
    c_m.wait()
    if not first:
        c_gm.wait()
        add_muscle(m, gain_m, sm, slot_parts)
    place = lax.broadcasted_iota(jnp.int32, (64, POINTS), 0)
    for c in range(8):
        rows = slice(c * 64, (c + 1) * 64)
        u = [m[s * CELLS + c * 64 : s * CELLS + (c + 1) * 64] for s in range(SPECIES)]
        near = [
            jnp.where(place == 0, 0.0, pltpu.roll(x, 1, 0))
            + jnp.where(place == 63, 0.0, pltpu.roll(x, 63, 0))
            for x in u
        ]
        for s, value in enumerate(local_rhs(u, near, None, deg[rows], MUSCLE_GAP)):
            stack(stacked, s, rows, value)
    finish(wm, tm, bm, SPECIES * SLOTS)
    outs.append(start(bm, store.at[MUSCLE_BASE : MUSCLE_BASE + SPECIES * CELLS]))
    outs.append(start(picks, store.at[PICKS : PICKS + 2 * SPECIES * SLOTS]))
    for s in range(SPECIES):
        for c in range(8):
            low, high = s * CELLS + c * 64, s * CELLS + c * 64 + 63
            muscle_ends[s * 16 + c : s * 16 + c + 1] = bm[low : low + 1]
            muscle_ends[s * 16 + 8 + c : s * 16 + 9 + c] = bm[high : high + 1]
    outs.append(start(muscle_ends, store.at[MUSCLE_ENDS : MUSCLE_ENDS + 48]))
    for copy in outs:
        copy.wait()


def f32(*shape):
    return jax.ShapeDtypeStruct(shape, jnp.float32)


def bf16(*shape):
    return jax.ShapeDtypeStruct(shape, jnp.bfloat16)


def call(kernel, name, args, far_in, outs, far_out, scratch, flops, moved, aliases):
    far = pl.BlockSpec(memory_space=pl.ANY)
    near = pl.BlockSpec(memory_space=pltpu.VMEM)
    return pl.pallas_call(
        kernel,
        out_shape=outs,
        in_specs=[far if i in far_in else near for i in range(len(args))],
        out_specs=[far if i in far_out else near for i in range(len(outs))],
        scratch_shapes=[pltpu.VMEM(a.shape, a.dtype) for a in scratch]
        + [pltpu.SemaphoreType.DMA((24,))],
        compiler_params=pltpu.CompilerParams(vmem_limit_bytes=VMEM_LIMIT),
        cost_estimate=pl.CostEstimate(flops=flops, bytes_accessed=moved, transcendentals=0),
        input_output_aliases=aliases,
        name=name,
    )(*args)


FIELD = f32(SPECIES * CELLS, POINTS)
LINEAR = f32(OWNERS * BLOCKS, POINTS)
STORE = f32(STORE_ROWS, POINTS)
ENDO_PARTS = bf16(ENDO_SLOTS, 2 * WIDE)
MUSCLE_PARTS = bf16(MUSCLE_SLOTS, 2 * WIDE)
SLOT_PARTS = bf16(SLOTS, 2 * WIDE)
ENDO_GAINS = f32(SPECIES * ENDO_SLOTS, POINTS)
MUSCLE_GAINS = f32(SPECIES * (SLOTS + 16), POINTS)
PICKED = f32(2 * SPECIES * SLOTS, POINTS)
EDGES = f32(SPECIES * 16, POINTS)
STACKED = bf16(SPECIES, CELLS, 2 * POINTS)
ENDO_STACK = bf16(SPECIES, ENDO_SLOTS, 2 * POINTS)
MUSCLE_STACK = bf16(SPECIES, MUSCLE_SLOTS, 2 * POINTS)
CELL_PARTS = bf16(CELLS, 2 * WIDE)
ENDO_END = f32(SPECIES, 128, POINTS)
MUSCLE_END = f32(SPECIES, 8, POINTS)
WEIGHT = bf16(SPECIES, 2 * POINTS, 2 * POINTS)
WEIGHT_ROW = bf16(SPECIES, POINTS, 2 * POINTS)
SLOT_SCRATCH = [ENDO_PARTS, MUSCLE_PARTS, ENDO_GAINS, MUSCLE_GAINS]


def first_call(*args):
    field = f32(SPECIES, CELLS, POINTS)
    pick = bf16(SLOTS, CELLS)
    return call(
        first_kernel, "first_rows", args, range(4), [LINEAR], range(1),
        [field, field, pick, pick, CELL_PARTS, LINEAR], 10**9, 3 * 10**6, {},
    )[0]


def post_call(*args):
    outs = [LINEAR, ENDO_END, ENDO_END, MUSCLE_END, MUSCLE_END, STORE]
    return call(
        post_kernel, "post", args, (0, 9), outs, (0, 5),
        [LINEAR, PICKED, f32(SPECIES * 256, POINTS), EDGES, LINEAR, *SLOT_SCRATCH, ENDO_STACK,
         MUSCLE_STACK, WEIGHT, WEIGHT],
        10**9, 5 * 10**6, {0: 0, 9: 5},
    )


def last_call(*args):
    return call(
        last_kernel, "last_step", args, (9,), [FIELD, FIELD], (0, 1),
        [FIELD, FIELD, *SLOT_SCRATCH, SLOT_PARTS, ENDO_STACK, MUSCLE_STACK, WEIGHT,
         WEIGHT],
        10**9, 5 * 10**6, {},
    )


def local_call(first, *args):
    outs = [STORE, WEIGHT_ROW, WEIGHT_ROW] if first else [STORE]
    return call(
        functools.partial(local_kernel, first), "local_part", args, (7, 8), outs, (0,),
        [FIELD, FIELD, ENDO_GAINS, MUSCLE_GAINS, FIELD, FIELD, PICKED, EDGES, STACKED,
         CELL_PARTS, SLOT_PARTS, f32(CELLS, POINTS), WEIGHT, WEIGHT],
        2 * 10**9, 8 * 10**6, {} if first else {7: 0},
    )


def one_hot(index, ends, slots):
    flat = index.T.reshape(-1)
    pad = jnp.full((slots - SLOTS - ends.size,), -1, jnp.int32)
    joined = jnp.concatenate([flat, ends, pad])
    cells = jnp.arange(CELLS, dtype=jnp.int32)
    spread = (cells[:, None] == flat[None, :]).astype(jnp.bfloat16)
    pick = (flat[:, None] == cells[None, :]).astype(jnp.bfloat16)
    wanted = jnp.concatenate([jnp.where(flat < 0, -2, flat), ends])
    passed = (wanted[:, None] == joined[None, :]).astype(jnp.bfloat16)
    return spread, pick, passed


def around(x, axis, step, closed):
    count = lax.axis_size(axis)
    pairs = [
        (i, (i + step) % count) for i in range(count) if closed or 0 <= i + step < count
    ]
    return lax.ppermute(x, axis, pairs)


def exchange(linear):
    out = lax.all_to_all(
        linear.reshape(OWNERS, BLOCKS // 2, 2, POINTS), DEVICES, split_axis=0, concat_axis=0,
        tiled=True,
    )
    return out.reshape(OWNERS * BLOCKS, POINTS)


def local(
    endothelium, muscle, agonist, proj_cell, proj_target, proj_count, endo_inverse, muscle_inverse
):
    e = endothelium.reshape(SPECIES, CELLS, POINTS)
    m = muscle.reshape(SPECIES, CELLS, POINTS)
    ag = agonist.reshape(CELLS, POINTS)
    slot_ids = jnp.arange(PAIR, dtype=jnp.int32)
    live = slot_ids[None, :] < proj_count[0][:, None]
    arrived = lax.all_to_all(
        jnp.where(live, proj_target[0], -1), DEVICES, split_axis=0, concat_axis=0, tiled=True
    )
    line = jnp.arange(128, dtype=jnp.int32)
    starts = jnp.arange(8, dtype=jnp.int32) * 64
    se, te, pe = one_hot(
        jnp.where(live, proj_cell[0], -1), jnp.concatenate([line, line + 384]), ENDO_SLOTS
    )
    sm, tm, pm = one_hot(arrived, jnp.concatenate([starts, starts + 63]), MUSCLE_SLOTS)
    e_top, e_bot = endothelium[:, 0], endothelium[:, 3]
    m_lo, m_hi = muscle[:, :, 0], muscle[:, :, 63]
    send = first_call(e, m, te, tm)
    store = None
    for step in range(TIME_STEPS):
        recv = exchange(send)
        halo = (
            around(e_bot, "ax", 1, False),
            around(e_top, "ax", -1, False),
            around(m_hi, "circ", 1, True),
            around(m_lo, "circ", -1, True),
        )
        if step == 0:
            store, we, wm = local_call(
                True, ag, se, sm, te, tm, endo_inverse, muscle_inverse,
                e.reshape(FIELD.shape), m.reshape(FIELD.shape),
            )
        else:
            (store,) = local_call(False, ag, se, sm, te, tm, we, wm, store)
        if step < TIME_STEPS - 1:
            send, e_top, e_bot, m_lo, m_hi, store = post_call(
                recv, *halo, we, wm, pe, pm, store
            )
        else:
            e, m = last_call(recv, *halo, we, wm, se, sm, store)
    return e.reshape(endothelium.shape), m.reshape(muscle.shape)


def solution(mesh):
    placed = (
        P(None, "ax", "circ", None),
        P(None, "ax", "circ", None),
        P("ax", "circ", None),
        P(("ax", "circ"), None, None),
        P(("ax", "circ"), None, None),
        P(("ax", "circ"), None),
        P(),
        P(),
    )
    return jax.shard_map(
        local,
        mesh=mesh,
        in_specs=placed,
        out_specs=(P(None, "ax", "circ", None), P(None, "ax", "circ", None)),
        check_vma=False,
    )
```

```python
import functools

import jax
import jax.numpy as jnp
from jax import lax
from jax.experimental import pallas as pl
from jax.experimental.pallas import tpu as pltpu
from jax.sharding import PartitionSpec as P

TIME_STEPS = 8
TIME_STEP = 0.2
COUPLING = (0.1, 0.3, 0.5)
ENDO_GAP = (0.05, 0.3, 0.5)
MUSCLE_GAP = (0.05, 0.1, 0.4)
DEVICES = ("ax", "circ")
PAIR = 2
SPECIES = 3
POINTS = 128
CELLS = 512
OWNERS = 128
HALF = SPECIES * PAIR
BLOCKS = 2 * HALF
SLOTS = PAIR * OWNERS
ENDO_SLOTS = SLOTS + 256
MUSCLE_SLOTS = SLOTS + 128
WIDE = SPECIES * POINTS
VMEM_LIMIT = 48 * 1024 * 1024
ENDO_BASE = 0
MUSCLE_BASE = ENDO_BASE + SPECIES * CELLS
PICKS = MUSCLE_BASE + SPECIES * CELLS
ENDO_GAIN = PICKS + 2 * SPECIES * SLOTS
MUSCLE_GAIN = ENDO_GAIN + SPECIES * ENDO_SLOTS
MUSCLE_ENDS = MUSCLE_GAIN + SPECIES * (SLOTS + 16)
STORE_ROWS = 34816


def col(i):
    return slice(i * POINTS, (i + 1) * POINTS)


def halves(x):
    hi = x.astype(jnp.bfloat16)
    lo = (x - hi.astype(jnp.float32)).astype(jnp.bfloat16)
    return hi, lo


def dot(a, b):
    return jnp.dot(a, b, preferred_element_type=jnp.float32)


def store_parts(parts, s, rows, value):
    hi, lo = halves(value)
    parts[rows, col(s)] = hi
    parts[rows, col(SPECIES + s)] = lo


def both(wide, s):
    return wide[:, col(s)] + wide[:, col(SPECIES + s)]


def slot_rows(base, s, k):
    return pl.ds(base + s * PAIR + k, OWNERS, stride=BLOCKS)


def local_rhs(u, near, drive, deg, gaps):
    decay = (0.6, 0.5, 0.8)
    square = u[1] * u[1]
    release = square / (0.5 + square)
    own = [
        u[s]
        * ((1.0 - TIME_STEP * (decay[s] + 2.0 * gaps[s])) - (TIME_STEP * COUPLING[s]) * deg)
        + (TIME_STEP * gaps[s]) * near[s]
        for s in range(SPECIES)
    ]
    own[0] = own[0] + (TIME_STEP * 1.2) * release - (TIME_STEP * 0.2) * u[2]
    if drive is not None:
        own[1] = own[1] + TIME_STEP * drive
    own[2] = own[2] + (TIME_STEP * 0.5) * u[0]
    return own


def stack(stacked, s, rows, value):
    hi, lo = halves(value)
    stacked[s, rows, 0:POINTS] = hi
    stacked[s, rows, POINTS:] = lo


def mover(sems):
    used = []

    def start(source, dest):
        copy = pltpu.make_async_copy(source, dest, sems.at[len(used)])
        used.append(copy)
        copy.start()
        return copy

    return start


def through(stacked, weight, gaps, parts, gain, count):
    for s in range(SPECIES):
        wide = dot(stacked[s], weight[s])
        value = wide[:, :POINTS] + wide[:, POINTS:]
        slots = value[:SLOTS] * (TIME_STEP * COUPLING[s])
        halo = value[SLOTS:] * (TIME_STEP * gaps[s])
        store_parts(parts, s, slice(0, SLOTS), slots)
        store_parts(parts, s, slice(SLOTS, parts.shape[0]), halo)
        gain[s * count : s * count + SLOTS] = slots
        gain[s * count + SLOTS : (s + 1) * count] = halo[: count - SLOTS]


def doubled(row, full):
    for s in range(SPECIES):
        full[s, 0:POINTS] = row[s]
        full[s, POINTS:] = row[s]


def split_inverse(inverse, row):
    for s in range(SPECIES):
        hi, lo = halves(inverse[s].T)
        row[s, :, 0:POINTS] = hi
        row[s, :, POINTS:] = lo


def endo_slots(recv, eu, ed, stacked):
    for s in range(SPECIES):
        for k in range(PAIR):
            rows = slice(k * OWNERS, (k + 1) * OWNERS)
            stack(stacked, s, rows, recv[slot_rows(HALF, s, k), :])
        stack(stacked, s, slice(SLOTS, SLOTS + 128), eu[s])
        stack(stacked, s, slice(SLOTS + 128, SLOTS + 256), ed[s])


def muscle_slots(recv, ml, mr, stacked):
    for s in range(SPECIES):
        for k in range(PAIR):
            rows = slice(k * OWNERS, (k + 1) * OWNERS)
            stack(stacked, s, rows, recv[slot_rows(0, s, k), :])
        both_ends = jnp.concatenate([ml[s], mr[s]], axis=0)
        stack(stacked, s, slice(SLOTS, SLOTS + 16), both_ends)
        stacked[s, SLOTS + 16 : MUSCLE_SLOTS, :] = jnp.zeros(
            (MUSCLE_SLOTS - SLOTS - 16, 2 * POINTS), jnp.bfloat16
        )


def first_kernel(e_h, m_h, te_h, tm_h, send_h, mlo, mhi, e, m, te, tm, parts, send, sems):
    start = mover(sems)
    into = [start(a, b) for a, b in ((e_h, e), (te_h, te), (m_h, m), (tm_h, tm))]
    for field, pick, base, ready in ((e, te, 0, into[:2]), (m, tm, HALF, into[2:])):
        for copy in ready:
            copy.wait()
        for s in range(SPECIES):
            store_parts(parts, s, slice(None), field[s])
        rows = dot(pick[...], parts[...])
        for s in range(SPECIES):
            value = both(rows, s)
            for k in range(PAIR):
                send[slot_rows(base, s, k), :] = value[k * OWNERS : (k + 1) * OWNERS]
    out = start(send, send_h)
    for s in range(SPECIES):
        for c in range(8):
            mlo[s, c : c + 1] = m[s, c * 64 : c * 64 + 1]
            mhi[s, c : c + 1] = m[s, c * 64 + 63 : c * 64 + 64]
    out.wait()


def add_endo(field, gain, spread, parts):
    for s in range(SPECIES):
        store_parts(parts, s, slice(None), gain[s * ENDO_SLOTS : s * ENDO_SLOTS + SLOTS])
    total = dot(spread[...], parts[...])
    for s in range(SPECIES):
        at = s * ENDO_SLOTS + SLOTS
        value = both(total, s)
        field[s * CELLS : s * CELLS + 128] += value[0:128] + gain[at : at + 128]
        field[s * CELLS + 128 : s * CELLS + 384] += value[128:384]
        field[s * CELLS + 384 : (s + 1) * CELLS] += value[384:] + gain[at + 128 : at + 256]


def add_muscle(field, gain, spread, parts):
    count = SLOTS + 16
    for s in range(SPECIES):
        store_parts(parts, s, slice(None), gain[s * count : s * count + SLOTS])
    total = dot(spread[...], parts[...])
    for s in range(SPECIES):
        field[s * CELLS : (s + 1) * CELLS] += both(total, s)
        for c in range(8):
            low, high = s * CELLS + c * 64, s * CELLS + c * 64 + 63
            at = s * count + SLOTS + c
            field[low : low + 1] += gain[at : at + 1]
            field[high : high + 1] += gain[at + 8 : at + 9]


def post_kernel(
    recv_h, eu, ed, ml, mr, we_row, wm_row, pe, pm, store_in,
    send_h, et, eb, mlo, mhi, store,
    recv, picks, ends, muscle_ends, send, ze, zm, gain_e, gain_m, stacked_e, stacked_m, we, wm,
    sems,
):
    start = mover(sems)
    c_recv = start(recv_h, recv)
    c_picks = start(store_in.at[PICKS : PICKS + 2 * SPECIES * SLOTS], picks)
    into = [start(store_in.at[MUSCLE_ENDS : MUSCLE_ENDS + 48], muscle_ends)]
    for s in range(SPECIES):
        for k, at in enumerate((0, 384)):
            row = ENDO_BASE + s * CELLS + at
            dest = (s * 2 + k) * 128
            into.append(start(store_in.at[row : row + 128], ends.at[dest : dest + 128]))
    outs = []
    doubled(we_row, we)
    doubled(wm_row, wm)
    c_recv.wait()
    endo_slots(recv, eu, ed, stacked_e)
    through(stacked_e, we, ENDO_GAP, ze, gain_e, ENDO_SLOTS)
    outs.append(start(gain_e, store.at[ENDO_GAIN : ENDO_GAIN + SPECIES * ENDO_SLOTS]))
    rows = dot(pe[0:SLOTS], ze[...])
    c_picks.wait()
    for s in range(SPECIES):
        value = both(rows, s) + picks[s * SLOTS : (s + 1) * SLOTS]
        for k in range(PAIR):
            send[slot_rows(0, s, k), :] = value[k * OWNERS : (k + 1) * OWNERS]
    muscle_slots(recv, ml, mr, stacked_m)
    through(stacked_m, wm, MUSCLE_GAP, zm, gain_m, SLOTS + 16)
    outs.append(start(gain_m, store.at[MUSCLE_GAIN : MUSCLE_GAIN + SPECIES * (SLOTS + 16)]))
    rows = dot(pm[...], zm[...])
    for copy in into:
        copy.wait()
    for s in range(SPECIES):
        value = both(rows, s)
        moved = value[:SLOTS] + picks[(SPECIES + s) * SLOTS : (SPECIES + s + 1) * SLOTS]
        for k in range(PAIR):
            send[slot_rows(HALF, s, k), :] = moved[k * OWNERS : (k + 1) * OWNERS]
        edge = value[SLOTS : SLOTS + 16] + muscle_ends[s * 16 : (s + 1) * 16]
        mlo[s] = edge[0:8]
        mhi[s] = edge[8:16]
    outs.append(start(send, send_h))
    rows = dot(pe[SLOTS:], ze[...])
    for s in range(SPECIES):
        value = both(rows, s)
        et[s] = value[:128] + ends[s * 256 : s * 256 + 128]
        eb[s] = value[128:] + ends[s * 256 + 128 : s * 256 + 256]
    for copy in outs:
        copy.wait()


def last_kernel(
    recv, eu, ed, ml, mr, we_row, wm_row, se, sm, store,
    e_h, m_h,
    e, m, ze, zm, gain_e, gain_m, parts, stacked_e, stacked_m, we, wm, sems,
):
    start = mover(sems)
    doubled(we_row, we)
    doubled(wm_row, wm)
    c_e = start(store.at[ENDO_BASE : ENDO_BASE + SPECIES * CELLS], e)
    c_m = start(store.at[MUSCLE_BASE : MUSCLE_BASE + SPECIES * CELLS], m)
    endo_slots(recv, eu, ed, stacked_e)
    through(stacked_e, we, ENDO_GAP, ze, gain_e, ENDO_SLOTS)
    c_e.wait()
    add_endo(e, gain_e, se, parts)
    out_e = start(e, e_h)
    muscle_slots(recv, ml, mr, stacked_m)
    through(stacked_m, wm, MUSCLE_GAP, zm, gain_m, SLOTS + 16)
    c_m.wait()
    add_muscle(m, gain_m, sm, parts)
    out_m = start(m, m_h)
    out_e.wait()
    out_m.wait()


def local_kernel(first, *refs):
    start = mover(refs[-1])
    (ag, se, sm, te, tm, we_row, wm_row), refs = refs[:7], refs[7:-1]
    if first:
        inverse_e, inverse_m = we_row, wm_row
        (e_h, m_h, store, we_row, wm_row, *refs) = refs
    else:
        (store_in, store, *refs) = refs
        e_h = store_in.at[ENDO_BASE : ENDO_BASE + SPECIES * CELLS]
        m_h = store_in.at[MUSCLE_BASE : MUSCLE_BASE + SPECIES * CELLS]
    (e, m, gain_e, gain_m, be, bm, picks, muscle_ends, stacked, parts, slot_parts, deg,
     we, wm) = refs
    c_e = start(e_h, e)
    if not first:
        c_ge = start(store_in.at[ENDO_GAIN : ENDO_GAIN + SPECIES * ENDO_SLOTS], gain_e)
    c_m = start(m_h, m)
    if not first:
        c_gm = start(store_in.at[MUSCLE_GAIN : MUSCLE_GAIN + SPECIES * (SLOTS + 16)], gain_m)
    if first:
        split_inverse(inverse_e, we_row)
        split_inverse(inverse_m, wm_row)
    doubled(we_row, we)
    doubled(wm_row, wm)
    ones = jnp.ones((SLOTS, POINTS), jnp.bfloat16)
    outs = []

    def finish(weight, pick, base, at):
        for s in range(SPECIES):
            wide = dot(stacked[s], weight[s])
            value = wide[:, :POINTS] + wide[:, POINTS:]
            base[s * CELLS : (s + 1) * CELLS] = value
            store_parts(parts, s, slice(None), value)
        rows = dot(pick[...], parts[...])
        for s in range(SPECIES):
            picks[at + s * SLOTS : at + (s + 1) * SLOTS] = both(rows, s)

    deg[...] = dot(se[...], ones)
    c_e.wait()
    if not first:
        c_ge.wait()
        add_endo(e, gain_e, se, slot_parts)
    for c in range(4):
        rows = slice(c * 128, (c + 1) * 128)
        u = [e[s * CELLS + c * 128 : s * CELLS + (c + 1) * 128] for s in range(SPECIES)]
        near = []
        for s in range(SPECIES):
            at = s * CELLS + c * 128
            sides = []
            if c > 0:
                sides.append(e[at - 128 : at])
            if c < 3:
                sides.append(e[at + 128 : at + 256])
            near.append(sides[0] + sides[1] if len(sides) == 2 else sides[0])
        for s, value in enumerate(local_rhs(u, near, ag[rows], deg[rows], ENDO_GAP)):
            stack(stacked, s, rows, value)
    finish(we, te, be, 0)
    outs.append(start(be, store.at[ENDO_BASE : ENDO_BASE + SPECIES * CELLS]))
    deg[...] = dot(sm[...], ones)
    c_m.wait()
    if not first:
        c_gm.wait()
        add_muscle(m, gain_m, sm, slot_parts)
    place = lax.broadcasted_iota(jnp.int32, (64, POINTS), 0)
    for c in range(8):
        rows = slice(c * 64, (c + 1) * 64)
        u = [m[s * CELLS + c * 64 : s * CELLS + (c + 1) * 64] for s in range(SPECIES)]
        near = [
            jnp.where(place == 0, 0.0, pltpu.roll(x, 1, 0))
            + jnp.where(place == 63, 0.0, pltpu.roll(x, 63, 0))
            for x in u
        ]
        for s, value in enumerate(local_rhs(u, near, None, deg[rows], MUSCLE_GAP)):
            stack(stacked, s, rows, value)
    finish(wm, tm, bm, SPECIES * SLOTS)
    outs.append(start(bm, store.at[MUSCLE_BASE : MUSCLE_BASE + SPECIES * CELLS]))
    outs.append(start(picks, store.at[PICKS : PICKS + 2 * SPECIES * SLOTS]))
    for s in range(SPECIES):
        for c in range(8):
            low, high = s * CELLS + c * 64, s * CELLS + c * 64 + 63
            muscle_ends[s * 16 + c : s * 16 + c + 1] = bm[low : low + 1]
            muscle_ends[s * 16 + 8 + c : s * 16 + 9 + c] = bm[high : high + 1]
    outs.append(start(muscle_ends, store.at[MUSCLE_ENDS : MUSCLE_ENDS + 48]))
    for copy in outs:
        copy.wait()


def f32(*shape):
    return jax.ShapeDtypeStruct(shape, jnp.float32)


def bf16(*shape):
    return jax.ShapeDtypeStruct(shape, jnp.bfloat16)


def call(kernel, name, args, far_in, outs, far_out, scratch, flops, moved, aliases):
    far = pl.BlockSpec(memory_space=pl.ANY)
    near = pl.BlockSpec(memory_space=pltpu.VMEM)
    return pl.pallas_call(
        kernel,
        out_shape=outs,
        in_specs=[far if i in far_in else near for i in range(len(args))],
        out_specs=[far if i in far_out else near for i in range(len(outs))],
        scratch_shapes=[pltpu.VMEM(a.shape, a.dtype) for a in scratch]
        + [pltpu.SemaphoreType.DMA((24,))],
        compiler_params=pltpu.CompilerParams(vmem_limit_bytes=VMEM_LIMIT),
        cost_estimate=pl.CostEstimate(flops=flops, bytes_accessed=moved, transcendentals=0),
        input_output_aliases=aliases,
        name=name,
    )(*args)


FIELD = f32(SPECIES * CELLS, POINTS)
LINEAR = f32(OWNERS * BLOCKS, POINTS)
STORE = f32(STORE_ROWS, POINTS)
ENDO_PARTS = bf16(ENDO_SLOTS, 2 * WIDE)
MUSCLE_PARTS = bf16(MUSCLE_SLOTS, 2 * WIDE)
SLOT_PARTS = bf16(SLOTS, 2 * WIDE)
ENDO_GAINS = f32(SPECIES * ENDO_SLOTS, POINTS)
MUSCLE_GAINS = f32(SPECIES * (SLOTS + 16), POINTS)
PICKED = f32(2 * SPECIES * SLOTS, POINTS)
EDGES = f32(SPECIES * 16, POINTS)
STACKED = bf16(SPECIES, CELLS, 2 * POINTS)
ENDO_STACK = bf16(SPECIES, ENDO_SLOTS, 2 * POINTS)
MUSCLE_STACK = bf16(SPECIES, MUSCLE_SLOTS, 2 * POINTS)
CELL_PARTS = bf16(CELLS, 2 * WIDE)
ENDO_END = f32(SPECIES, 128, POINTS)
MUSCLE_END = f32(SPECIES, 8, POINTS)
WEIGHT = bf16(SPECIES, 2 * POINTS, 2 * POINTS)
WEIGHT_ROW = bf16(SPECIES, POINTS, 2 * POINTS)
SLOT_SCRATCH = [ENDO_PARTS, MUSCLE_PARTS, ENDO_GAINS, MUSCLE_GAINS]


def first_call(*args):
    field = f32(SPECIES, CELLS, POINTS)
    pick = bf16(SLOTS, CELLS)
    return call(
        first_kernel, "first_rows", args, range(4), [LINEAR, MUSCLE_END, MUSCLE_END], range(1),
        [field, field, pick, pick, CELL_PARTS, LINEAR], 10**9, 3 * 10**6, {},
    )


def post_call(*args):
    outs = [LINEAR, ENDO_END, ENDO_END, MUSCLE_END, MUSCLE_END, STORE]
    return call(
        post_kernel, "post", args, (0, 9), outs, (0, 5),
        [LINEAR, PICKED, f32(SPECIES * 256, POINTS), EDGES, LINEAR, *SLOT_SCRATCH, ENDO_STACK,
         MUSCLE_STACK, WEIGHT, WEIGHT],
        10**9, 5 * 10**6, {0: 0, 9: 5},
    )


def last_call(*args):
    return call(
        last_kernel, "last_step", args, (9,), [FIELD, FIELD], (0, 1),
        [FIELD, FIELD, *SLOT_SCRATCH, SLOT_PARTS, ENDO_STACK, MUSCLE_STACK, WEIGHT,
         WEIGHT],
        10**9, 5 * 10**6, {},
    )


def local_call(first, *args):
    outs = [STORE, WEIGHT_ROW, WEIGHT_ROW] if first else [STORE]
    return call(
        functools.partial(local_kernel, first), "local_part", args, (7, 8), outs, (0,),
        [FIELD, FIELD, ENDO_GAINS, MUSCLE_GAINS, FIELD, FIELD, PICKED, EDGES, STACKED,
         CELL_PARTS, SLOT_PARTS, f32(CELLS, POINTS), WEIGHT, WEIGHT],
        2 * 10**9, 8 * 10**6, {} if first else {7: 0},
    )


def one_hot(index, ends, slots):
    flat = index.T.reshape(-1)
    pad = jnp.full((slots - SLOTS - ends.size,), -1, jnp.int32)
    joined = jnp.concatenate([flat, ends, pad])
    cells = jnp.arange(CELLS, dtype=jnp.int32)
    spread = (cells[:, None] == flat[None, :]).astype(jnp.bfloat16)
    pick = (flat[:, None] == cells[None, :]).astype(jnp.bfloat16)
    wanted = jnp.concatenate([jnp.where(flat < 0, -2, flat), ends])
    passed = (wanted[:, None] == joined[None, :]).astype(jnp.bfloat16)
    return spread, pick, passed


def around(x, axis, step, closed):
    count = lax.axis_size(axis)
    pairs = [
        (i, (i + step) % count) for i in range(count) if closed or 0 <= i + step < count
    ]
    return lax.ppermute(x, axis, pairs)


def exchange(linear):
    out = lax.all_to_all(
        linear.reshape(OWNERS, BLOCKS // 2, 2, POINTS), DEVICES, split_axis=0, concat_axis=0,
        tiled=True,
    )
    return out.reshape(OWNERS * BLOCKS, POINTS)


def local(
    endothelium, muscle, agonist, proj_cell, proj_target, proj_count, endo_inverse, muscle_inverse
):
    e = endothelium.reshape(SPECIES, CELLS, POINTS)
    m = muscle.reshape(SPECIES, CELLS, POINTS)
    ag = agonist.reshape(CELLS, POINTS)
    slot_ids = jnp.arange(PAIR, dtype=jnp.int32)
    live = slot_ids[None, :] < proj_count[0][:, None]
    arrived = lax.all_to_all(
        jnp.where(live, proj_target[0], -1), DEVICES, split_axis=0, concat_axis=0, tiled=True
    )
    line = jnp.arange(128, dtype=jnp.int32)
    starts = jnp.arange(8, dtype=jnp.int32) * 64
    se, te, pe = one_hot(
        jnp.where(live, proj_cell[0], -1), jnp.concatenate([line, line + 384]), ENDO_SLOTS
    )
    sm, tm, pm = one_hot(arrived, jnp.concatenate([starts, starts + 63]), MUSCLE_SLOTS)
    e_top, e_bot = endothelium[:, 0], endothelium[:, 3]
    send, m_lo, m_hi = first_call(e, m, te, tm)
    store = None
    for step in range(TIME_STEPS):
        recv = exchange(send)
        halo = (
            around(e_bot, "ax", 1, False),
            around(e_top, "ax", -1, False),
            around(m_hi, "circ", 1, True),
            around(m_lo, "circ", -1, True),
        )
        if step == 0:
            store, we, wm = local_call(
                True, ag, se, sm, te, tm, endo_inverse, muscle_inverse,
                e.reshape(FIELD.shape), m.reshape(FIELD.shape),
            )
        else:
            (store,) = local_call(False, ag, se, sm, te, tm, we, wm, store)
        if step < TIME_STEPS - 1:
            send, e_top, e_bot, m_lo, m_hi, store = post_call(
                recv, *halo, we, wm, pe, pm, store
            )
        else:
            e, m = last_call(recv, *halo, we, wm, se, sm, store)
    return e.reshape(endothelium.shape), m.reshape(muscle.shape)


def solution(mesh):
    placed = (
        P(None, "ax", "circ", None),
        P(None, "ax", "circ", None),
        P("ax", "circ", None),
        P(("ax", "circ"), None, None),
        P(("ax", "circ"), None, None),
        P(("ax", "circ"), None),
        P(),
        P(),
    )
    return jax.shard_map(
        local,
        mesh=mesh,
        in_specs=placed,
        out_specs=(P(None, "ax", "circ", None), P(None, "ax", "circ", None)),
        check_vma=False,
    )
```

```python
import functools

import jax
import jax.numpy as jnp
from jax import lax
from jax.experimental import pallas as pl
from jax.experimental.pallas import tpu as pltpu
from jax.sharding import PartitionSpec as P

TIME_STEPS = 8
TIME_STEP = 0.2
COUPLING = (0.1, 0.3, 0.5)
ENDO_GAP = (0.05, 0.3, 0.5)
MUSCLE_GAP = (0.05, 0.1, 0.4)
DEVICES = ("ax", "circ")
PAIR = 2
SPECIES = 3
POINTS = 128
CELLS = 512
OWNERS = 128
HALF = SPECIES * PAIR
BLOCKS = 2 * HALF
SLOTS = PAIR * OWNERS
ENDO_SLOTS = SLOTS + 256
MUSCLE_SLOTS = SLOTS + 128
WIDE = SPECIES * POINTS
VMEM_LIMIT = 48 * 1024 * 1024
ENDO_BASE = 0
MUSCLE_BASE = ENDO_BASE + SPECIES * CELLS
PICKS = MUSCLE_BASE + SPECIES * CELLS
ENDO_GAIN = PICKS + 2 * SPECIES * SLOTS
MUSCLE_GAIN = ENDO_GAIN + SPECIES * ENDO_SLOTS
MUSCLE_ENDS = MUSCLE_GAIN + SPECIES * (SLOTS + 16)
STORE_ROWS = 34816


def col(i):
    return slice(i * POINTS, (i + 1) * POINTS)


def halves(x):
    hi = x.astype(jnp.bfloat16)
    lo = (x - hi.astype(jnp.float32)).astype(jnp.bfloat16)
    return hi, lo


def dot(a, b):
    return jnp.dot(a, b, preferred_element_type=jnp.float32)


def store_parts(parts, s, rows, value):
    hi, lo = halves(value)
    parts[rows, col(s)] = hi
    parts[rows, col(SPECIES + s)] = lo


def both(wide, s):
    return wide[:, col(s)] + wide[:, col(SPECIES + s)]


def slot_rows(base, s, k):
    return pl.ds(base + s * PAIR + k, OWNERS, stride=BLOCKS)


def local_rhs(u, near, drive, deg, gaps):
    decay = (0.6, 0.5, 0.8)
    square = u[1] * u[1]
    release = square / (0.5 + square)
    own = [
        u[s]
        * ((1.0 - TIME_STEP * (decay[s] + 2.0 * gaps[s])) - (TIME_STEP * COUPLING[s]) * deg)
        + (TIME_STEP * gaps[s]) * near[s]
        for s in range(SPECIES)
    ]
    own[0] = own[0] + (TIME_STEP * 1.2) * release - (TIME_STEP * 0.2) * u[2]
    if drive is not None:
        own[1] = own[1] + TIME_STEP * drive
    own[2] = own[2] + (TIME_STEP * 0.5) * u[0]
    return own


def stack(stacked, s, rows, value):
    hi, lo = halves(value)
    stacked[s, rows, 0:POINTS] = hi
    stacked[s, rows, POINTS:] = lo


def mover(sems):
    used = []

    def start(source, dest):
        copy = pltpu.make_async_copy(source, dest, sems.at[len(used)])
        used.append(copy)
        copy.start()
        return copy

    return start


def through(stacked, weight, gaps, parts, gain, count):
    for s in range(SPECIES):
        wide = dot(stacked[s], weight[s])
        value = wide[:, :POINTS] + wide[:, POINTS:]
        slots = value[:SLOTS] * (TIME_STEP * COUPLING[s])
        halo = value[SLOTS:] * (TIME_STEP * gaps[s])
        store_parts(parts, s, slice(0, SLOTS), slots)
        store_parts(parts, s, slice(SLOTS, parts.shape[0]), halo)
        gain[s * count : s * count + SLOTS] = slots
        gain[s * count + SLOTS : (s + 1) * count] = halo[: count - SLOTS]


def doubled(row, full):
    for s in range(SPECIES):
        full[s, 0:POINTS] = row[s]
        full[s, POINTS:] = row[s]


def split_inverse(inverse, row):
    for s in range(SPECIES):
        hi, lo = halves(inverse[s].T)
        row[s, :, 0:POINTS] = hi
        row[s, :, POINTS:] = lo


def endo_slots(recv, eu, ed, stacked):
    for s in range(SPECIES):
        for k in range(PAIR):
            rows = slice(k * OWNERS, (k + 1) * OWNERS)
            stack(stacked, s, rows, recv[slot_rows(HALF, s, k), :])
        stack(stacked, s, slice(SLOTS, SLOTS + 128), eu[s])
        stack(stacked, s, slice(SLOTS + 128, SLOTS + 256), ed[s])


def muscle_slots(recv, ml, mr, stacked):
    for s in range(SPECIES):
        for k in range(PAIR):
            rows = slice(k * OWNERS, (k + 1) * OWNERS)
            stack(stacked, s, rows, recv[slot_rows(0, s, k), :])
        both_ends = jnp.concatenate([ml[s], mr[s]], axis=0)
        stack(stacked, s, slice(SLOTS, SLOTS + 16), both_ends)
        stacked[s, SLOTS + 16 : MUSCLE_SLOTS, :] = jnp.zeros(
            (MUSCLE_SLOTS - SLOTS - 16, 2 * POINTS), jnp.bfloat16
        )


def first_kernel(e_h, m_h, te_h, tm_h, send_h, mlo, mhi, e, m, te, tm, parts, send, sems):
    start = mover(sems)
    into = [start(a, b) for a, b in ((e_h, e), (te_h, te), (m_h, m), (tm_h, tm))]
    for field, pick, base, ready in ((e, te, 0, into[:2]), (m, tm, HALF, into[2:])):
        for copy in ready:
            copy.wait()
        for s in range(SPECIES):
            store_parts(parts, s, slice(None), field[s])
        rows = dot(pick[...], parts[...])
        for s in range(SPECIES):
            value = both(rows, s)
            for k in range(PAIR):
                send[slot_rows(base, s, k), :] = value[k * OWNERS : (k + 1) * OWNERS]
    out = start(send, send_h)
    for s in range(SPECIES):
        for c in range(8):
            mlo[s, c : c + 1] = m[s, c * 64 : c * 64 + 1]
            mhi[s, c : c + 1] = m[s, c * 64 + 63 : c * 64 + 64]
    out.wait()


def add_endo(field, gain, spread, parts):
    for s in range(SPECIES):
        store_parts(parts, s, slice(None), gain[s * ENDO_SLOTS : s * ENDO_SLOTS + SLOTS])
    total = dot(spread[...], parts[...])
    for s in range(SPECIES):
        at = s * ENDO_SLOTS + SLOTS
        value = both(total, s)
        field[s * CELLS : s * CELLS + 128] += value[0:128] + gain[at : at + 128]
        field[s * CELLS + 128 : s * CELLS + 384] += value[128:384]
        field[s * CELLS + 384 : (s + 1) * CELLS] += value[384:] + gain[at + 128 : at + 256]


def add_muscle(field, gain, spread, parts):
    count = SLOTS + 16
    for s in range(SPECIES):
        store_parts(parts, s, slice(None), gain[s * count : s * count + SLOTS])
    total = dot(spread[...], parts[...])
    for s in range(SPECIES):
        field[s * CELLS : (s + 1) * CELLS] += both(total, s)
        for c in range(8):
            low, high = s * CELLS + c * 64, s * CELLS + c * 64 + 63
            at = s * count + SLOTS + c
            field[low : low + 1] += gain[at : at + 1]
            field[high : high + 1] += gain[at + 8 : at + 9]


def post_kernel(
    recv_h, eu, ed, ml, mr, we_row, wm_row, pe, pm, store_in,
    send_h, et, eb, mlo, mhi, store,
    recv, picks, ends, muscle_ends, send, ze, zm, gain_e, gain_m, stacked_e, stacked_m, we, wm,
    sems,
):
    start = mover(sems)
    c_recv = start(recv_h, recv)
    c_picks = start(store_in.at[PICKS : PICKS + 2 * SPECIES * SLOTS], picks)
    into = [start(store_in.at[MUSCLE_ENDS : MUSCLE_ENDS + 48], muscle_ends)]
    for s in range(SPECIES):
        for k, at in enumerate((0, 384)):
            row = ENDO_BASE + s * CELLS + at
            dest = (s * 2 + k) * 128
            into.append(start(store_in.at[row : row + 128], ends.at[dest : dest + 128]))
    outs = []
    doubled(we_row, we)
    doubled(wm_row, wm)
    c_recv.wait()
    endo_slots(recv, eu, ed, stacked_e)
    through(stacked_e, we, ENDO_GAP, ze, gain_e, ENDO_SLOTS)
    outs.append(start(gain_e, store.at[ENDO_GAIN : ENDO_GAIN + SPECIES * ENDO_SLOTS]))
    rows = dot(pe[0:SLOTS], ze[...])
    c_picks.wait()
    for s in range(SPECIES):
        value = both(rows, s) + picks[s * SLOTS : (s + 1) * SLOTS]
        for k in range(PAIR):
            send[slot_rows(0, s, k), :] = value[k * OWNERS : (k + 1) * OWNERS]
    muscle_slots(recv, ml, mr, stacked_m)
    through(stacked_m, wm, MUSCLE_GAP, zm, gain_m, SLOTS + 16)
    outs.append(start(gain_m, store.at[MUSCLE_GAIN : MUSCLE_GAIN + SPECIES * (SLOTS + 16)]))
    rows = dot(pm[...], zm[...])
    for copy in into:
        copy.wait()
    for s in range(SPECIES):
        value = both(rows, s)
        moved = value[:SLOTS] + picks[(SPECIES + s) * SLOTS : (SPECIES + s + 1) * SLOTS]
        for k in range(PAIR):
            send[slot_rows(HALF, s, k), :] = moved[k * OWNERS : (k + 1) * OWNERS]
        edge = value[SLOTS : SLOTS + 16] + muscle_ends[s * 16 : (s + 1) * 16]
        mlo[s] = edge[0:8]
        mhi[s] = edge[8:16]
    outs.append(start(send, send_h))
    rows = dot(pe[SLOTS:], ze[...])
    for s in range(SPECIES):
        value = both(rows, s)
        et[s] = value[:128] + ends[s * 256 : s * 256 + 128]
        eb[s] = value[128:] + ends[s * 256 + 128 : s * 256 + 256]
    for copy in outs:
        copy.wait()


def last_kernel(
    recv_h, eu, ed, ml, mr, we_row, wm_row, se, sm, store,
    e_h, m_h,
    recv, e, m, ze, zm, gain_e, gain_m, parts, stacked_e, stacked_m, we, wm, sems,
):
    start = mover(sems)
    c_recv = start(recv_h, recv)
    doubled(we_row, we)
    doubled(wm_row, wm)
    c_e = start(store.at[ENDO_BASE : ENDO_BASE + SPECIES * CELLS], e)
    c_m = start(store.at[MUSCLE_BASE : MUSCLE_BASE + SPECIES * CELLS], m)
    c_recv.wait()
    endo_slots(recv, eu, ed, stacked_e)
    through(stacked_e, we, ENDO_GAP, ze, gain_e, ENDO_SLOTS)
    c_e.wait()
    add_endo(e, gain_e, se, parts)
    out_e = start(e, e_h)
    muscle_slots(recv, ml, mr, stacked_m)
    through(stacked_m, wm, MUSCLE_GAP, zm, gain_m, SLOTS + 16)
    c_m.wait()
    add_muscle(m, gain_m, sm, parts)
    out_m = start(m, m_h)
    out_e.wait()
    out_m.wait()


def local_kernel(first, *refs):
    start = mover(refs[-1])
    (ag, se, sm, te, tm, we_row, wm_row), refs = refs[:7], refs[7:-1]
    if first:
        inverse_e, inverse_m = we_row, wm_row
        (e_h, m_h, store, we_row, wm_row, *refs) = refs
    else:
        (store_in, store, *refs) = refs
        e_h = store_in.at[ENDO_BASE : ENDO_BASE + SPECIES * CELLS]
        m_h = store_in.at[MUSCLE_BASE : MUSCLE_BASE + SPECIES * CELLS]
    (e, m, gain_e, gain_m, be, bm, picks, muscle_ends, stacked, parts, slot_parts, deg,
     we, wm) = refs
    c_e = start(e_h, e)
    if not first:
        c_ge = start(store_in.at[ENDO_GAIN : ENDO_GAIN + SPECIES * ENDO_SLOTS], gain_e)
    c_m = start(m_h, m)
    if not first:
        c_gm = start(store_in.at[MUSCLE_GAIN : MUSCLE_GAIN + SPECIES * (SLOTS + 16)], gain_m)
    if first:
        split_inverse(inverse_e, we_row)
        split_inverse(inverse_m, wm_row)
    doubled(we_row, we)
    doubled(wm_row, wm)
    ones = jnp.ones((SLOTS, POINTS), jnp.bfloat16)
    outs = []

    def finish(weight, pick, base, at):
        for s in range(SPECIES):
            wide = dot(stacked[s], weight[s])
            value = wide[:, :POINTS] + wide[:, POINTS:]
            base[s * CELLS : (s + 1) * CELLS] = value
            store_parts(parts, s, slice(None), value)
        rows = dot(pick[...], parts[...])
        for s in range(SPECIES):
            picks[at + s * SLOTS : at + (s + 1) * SLOTS] = both(rows, s)

    deg[...] = dot(se[...], ones)
    c_e.wait()
    if not first:
        c_ge.wait()
        add_endo(e, gain_e, se, slot_parts)
    for c in range(4):
        rows = slice(c * 128, (c + 1) * 128)
        u = [e[s * CELLS + c * 128 : s * CELLS + (c + 1) * 128] for s in range(SPECIES)]
        near = []
        for s in range(SPECIES):
            at = s * CELLS + c * 128
            sides = []
            if c > 0:
                sides.append(e[at - 128 : at])
            if c < 3:
                sides.append(e[at + 128 : at + 256])
            near.append(sides[0] + sides[1] if len(sides) == 2 else sides[0])
        for s, value in enumerate(local_rhs(u, near, ag[rows], deg[rows], ENDO_GAP)):
            stack(stacked, s, rows, value)
    finish(we, te, be, 0)
    outs.append(start(be, store.at[ENDO_BASE : ENDO_BASE + SPECIES * CELLS]))
    deg[...] = dot(sm[...], ones)
    c_m.wait()
    if not first:
        c_gm.wait()
        add_muscle(m, gain_m, sm, slot_parts)
    place = lax.broadcasted_iota(jnp.int32, (64, POINTS), 0)
    for c in range(8):
        rows = slice(c * 64, (c + 1) * 64)
        u = [m[s * CELLS + c * 64 : s * CELLS + (c + 1) * 64] for s in range(SPECIES)]
        near = [
            jnp.where(place == 0, 0.0, pltpu.roll(x, 1, 0))
            + jnp.where(place == 63, 0.0, pltpu.roll(x, 63, 0))
            for x in u
        ]
        for s, value in enumerate(local_rhs(u, near, None, deg[rows], MUSCLE_GAP)):
            stack(stacked, s, rows, value)
    finish(wm, tm, bm, SPECIES * SLOTS)
    outs.append(start(bm, store.at[MUSCLE_BASE : MUSCLE_BASE + SPECIES * CELLS]))
    outs.append(start(picks, store.at[PICKS : PICKS + 2 * SPECIES * SLOTS]))
    for s in range(SPECIES):
        for c in range(8):
            low, high = s * CELLS + c * 64, s * CELLS + c * 64 + 63
            muscle_ends[s * 16 + c : s * 16 + c + 1] = bm[low : low + 1]
            muscle_ends[s * 16 + 8 + c : s * 16 + 9 + c] = bm[high : high + 1]
    outs.append(start(muscle_ends, store.at[MUSCLE_ENDS : MUSCLE_ENDS + 48]))
    for copy in outs:
        copy.wait()


def f32(*shape):
    return jax.ShapeDtypeStruct(shape, jnp.float32)


def bf16(*shape):
    return jax.ShapeDtypeStruct(shape, jnp.bfloat16)


def call(kernel, name, args, far_in, outs, far_out, scratch, flops, moved, aliases):
    far = pl.BlockSpec(memory_space=pl.ANY)
    near = pl.BlockSpec(memory_space=pltpu.VMEM)
    return pl.pallas_call(
        kernel,
        out_shape=outs,
        in_specs=[far if i in far_in else near for i in range(len(args))],
        out_specs=[far if i in far_out else near for i in range(len(outs))],
        scratch_shapes=[pltpu.VMEM(a.shape, a.dtype) for a in scratch]
        + [pltpu.SemaphoreType.DMA((24,))],
        compiler_params=pltpu.CompilerParams(vmem_limit_bytes=VMEM_LIMIT),
        cost_estimate=pl.CostEstimate(flops=flops, bytes_accessed=moved, transcendentals=0),
        input_output_aliases=aliases,
        name=name,
    )(*args)


FIELD = f32(SPECIES * CELLS, POINTS)
LINEAR = f32(OWNERS * BLOCKS, POINTS)
STORE = f32(STORE_ROWS, POINTS)
ENDO_PARTS = bf16(ENDO_SLOTS, 2 * WIDE)
MUSCLE_PARTS = bf16(MUSCLE_SLOTS, 2 * WIDE)
SLOT_PARTS = bf16(SLOTS, 2 * WIDE)
ENDO_GAINS = f32(SPECIES * ENDO_SLOTS, POINTS)
MUSCLE_GAINS = f32(SPECIES * (SLOTS + 16), POINTS)
PICKED = f32(2 * SPECIES * SLOTS, POINTS)
EDGES = f32(SPECIES * 16, POINTS)
STACKED = bf16(SPECIES, CELLS, 2 * POINTS)
ENDO_STACK = bf16(SPECIES, ENDO_SLOTS, 2 * POINTS)
MUSCLE_STACK = bf16(SPECIES, MUSCLE_SLOTS, 2 * POINTS)
CELL_PARTS = bf16(CELLS, 2 * WIDE)
ENDO_END = f32(SPECIES, 128, POINTS)
MUSCLE_END = f32(SPECIES, 8, POINTS)
WEIGHT = bf16(SPECIES, 2 * POINTS, 2 * POINTS)
WEIGHT_ROW = bf16(SPECIES, POINTS, 2 * POINTS)
SLOT_SCRATCH = [ENDO_PARTS, MUSCLE_PARTS, ENDO_GAINS, MUSCLE_GAINS]


def first_call(*args):
    field = f32(SPECIES, CELLS, POINTS)
    pick = bf16(SLOTS, CELLS)
    return call(
        first_kernel, "first_rows", args, range(4), [LINEAR, MUSCLE_END, MUSCLE_END], range(1),
        [field, field, pick, pick, CELL_PARTS, LINEAR], 10**9, 3 * 10**6, {},
    )


def post_call(*args):
    outs = [LINEAR, ENDO_END, ENDO_END, MUSCLE_END, MUSCLE_END, STORE]
    return call(
        post_kernel, "post", args, (0, 9), outs, (0, 5),
        [LINEAR, PICKED, f32(SPECIES * 256, POINTS), EDGES, LINEAR, *SLOT_SCRATCH, ENDO_STACK,
         MUSCLE_STACK, WEIGHT, WEIGHT],
        10**9, 5 * 10**6, {0: 0, 9: 5},
    )


def last_call(*args):
    return call(
        last_kernel, "last_step", args, (0, 9), [FIELD, FIELD], (0, 1),
        [LINEAR, FIELD, FIELD, *SLOT_SCRATCH, SLOT_PARTS, ENDO_STACK, MUSCLE_STACK, WEIGHT,
         WEIGHT],
        10**9, 5 * 10**6, {},
    )


def local_call(first, *args):
    outs = [STORE, WEIGHT_ROW, WEIGHT_ROW] if first else [STORE]
    return call(
        functools.partial(local_kernel, first), "local_part", args, (7, 8), outs, (0,),
        [FIELD, FIELD, ENDO_GAINS, MUSCLE_GAINS, FIELD, FIELD, PICKED, EDGES, STACKED,
         CELL_PARTS, SLOT_PARTS, f32(CELLS, POINTS), WEIGHT, WEIGHT],
        2 * 10**9, 8 * 10**6, {} if first else {7: 0},
    )


def one_hot(index, ends, slots):
    flat = index.T.reshape(-1)
    pad = jnp.full((slots - SLOTS - ends.size,), -1, jnp.int32)
    joined = jnp.concatenate([flat, ends, pad])
    cells = jnp.arange(CELLS, dtype=jnp.int32)
    spread = (cells[:, None] == flat[None, :]).astype(jnp.bfloat16)
    pick = (flat[:, None] == cells[None, :]).astype(jnp.bfloat16)
    wanted = jnp.concatenate([jnp.where(flat < 0, -2, flat), ends])
    passed = (wanted[:, None] == joined[None, :]).astype(jnp.bfloat16)
    return spread, pick, passed


def around(x, axis, step, closed):
    count = lax.axis_size(axis)
    pairs = [
        (i, (i + step) % count) for i in range(count) if closed or 0 <= i + step < count
    ]
    return lax.ppermute(x, axis, pairs)


def exchange(linear):
    out = lax.all_to_all(
        linear.reshape(OWNERS, BLOCKS // 2, 2, POINTS), DEVICES, split_axis=0, concat_axis=0,
        tiled=True,
    )
    return out.reshape(OWNERS * BLOCKS, POINTS)


def local(
    endothelium, muscle, agonist, proj_cell, proj_target, proj_count, endo_inverse, muscle_inverse
):
    e = endothelium.reshape(SPECIES, CELLS, POINTS)
    m = muscle.reshape(SPECIES, CELLS, POINTS)
    ag = agonist.reshape(CELLS, POINTS)
    slot_ids = jnp.arange(PAIR, dtype=jnp.int32)
    live = slot_ids[None, :] < proj_count[0][:, None]
    arrived = lax.all_to_all(
        jnp.where(live, proj_target[0], -1), DEVICES, split_axis=0, concat_axis=0, tiled=True
    )
    line = jnp.arange(128, dtype=jnp.int32)
    starts = jnp.arange(8, dtype=jnp.int32) * 64
    se, te, pe = one_hot(
        jnp.where(live, proj_cell[0], -1), jnp.concatenate([line, line + 384]), ENDO_SLOTS
    )
    sm, tm, pm = one_hot(arrived, jnp.concatenate([starts, starts + 63]), MUSCLE_SLOTS)
    e_top, e_bot = endothelium[:, 0], endothelium[:, 3]
    send, m_lo, m_hi = first_call(e, m, te, tm)
    store = None
    for step in range(TIME_STEPS):
        recv = exchange(send)
        halo = (
            around(e_bot, "ax", 1, False),
            around(e_top, "ax", -1, False),
            around(m_hi, "circ", 1, True),
            around(m_lo, "circ", -1, True),
        )
        if step == 0:
            store, we, wm = local_call(
                True, ag, se, sm, te, tm, endo_inverse, muscle_inverse,
                e.reshape(FIELD.shape), m.reshape(FIELD.shape),
            )
        else:
            (store,) = local_call(False, ag, se, sm, te, tm, we, wm, store)
        if step < TIME_STEPS - 1:
            send, e_top, e_bot, m_lo, m_hi, store = post_call(
                recv, *halo, we, wm, pe, pm, store
            )
        else:
            e, m = last_call(recv, *halo, we, wm, se, sm, store)
    return e.reshape(endothelium.shape), m.reshape(muscle.shape)


def solution(mesh):
    placed = (
        P(None, "ax", "circ", None),
        P(None, "ax", "circ", None),
        P("ax", "circ", None),
        P(("ax", "circ"), None, None),
        P(("ax", "circ"), None, None),
        P(("ax", "circ"), None),
        P(),
        P(),
    )
    return jax.shard_map(
        local,
        mesh=mesh,
        in_specs=placed,
        out_specs=(P(None, "ax", "circ", None), P(None, "ax", "circ", None)),
        check_vma=False,
    )
```
